1024 devices in a mesh: dp: 32 (over z, core), node: 4 (over x), innode: 8 (over y).
Axes of the slice: x: 4, y: 8, z: 16, core: 2. Of those that a mesh axis runs over, the one named last changes fastest.
Arguments:
- tokens: bfloat16 [16384, 2048], P(('dp', 'node')), may hold values from -6 to 6
- routes: int32 [16384, 6], P(('dp', 'node')), may hold values from 0 to 31, as said below
- route_gates: float32 [16384, 6], P(('dp', 'node')), may hold values from 0.1 to 1
- out_grad: bfloat16 [16384, 2048], P(('dp', 'node')), may hold values from -4 to 4
- gate_weight: bfloat16 [32, 2048, 768], P(('node', 'innode'), 'dp'), may hold values from -0.125 to 0.125
- up_weight: bfloat16 [32, 2048, 768], P(('node', 'innode'), 'dp'), may hold values from -0.125 to 0.125
- down_weight: bfloat16 [32, 2048, 768], P(('node', 'innode'), 'dp'), may hold values from -0.21875 to 0.21875
Outputs:
- token_grad: bfloat16 [16384, 2048], P(('dp', 'node', 'innode'))
The draws below stay inside these ranges and needn't reach their ends.
Inputs may be any that keep to these rules, and one draw needn't show every extreme that they name: `routes`: each row names 6 different experts, 3 in each of 2 different groups, the group of expert e being e // 8. In aligned blocks of 128 rows every group is named by the same number of rows, and no expert is named by more than 24 rows, a bound that some expert meets in every block.
All inputs are finite; a program needn't handle non-finite values.
Results may differ from the reference program's by a relative error of at most 0.015.
Values may be sent and summed in bfloat16 or wider, within the bound.
A program may use at most 64 MiB of HBM per device.

```python
import jax
import jax.numpy as jnp
from jax import lax

D = 2048
W = 768
TOP = 6
TOK_DEV = 128
PER_NODE = 3
EXPERTS = 32
CAP = 24
TOKENS = 16384
N_NODE = 4
N_INNODE = 8


def draw_routes(key, part):
    key = jax.random.fold_in(key, 7)
    blocks = TOKENS // TOK_DEV
    node_key, inner_key, order_key, step_key = jax.random.split(key, 4)
    steps = jax.random.randint(step_key, (blocks, 1, 1), 1, N_NODE).astype(jnp.int32)
    token_pos = jnp.arange(TOK_DEV, dtype=jnp.int32)[None, :, None]
    slot_pos = jnp.arange(TOP, dtype=jnp.int32)[None, None, :]
    side = slot_pos // PER_NODE
    place = slot_pos % PER_NODE
    share = TOK_DEV // N_NODE
    node_raw = (token_pos % N_NODE + side * steps) % N_NODE
    rank = side * share + token_pos // N_NODE
    inner_raw = jnp.broadcast_to((PER_NODE * rank + place) % N_INNODE, node_raw.shape)
    node_perm = jax.vmap(lambda k: jax.random.permutation(k, N_NODE))(jax.random.split(node_key, blocks)).astype(jnp.int32)
    inner_perm = jax.vmap(lambda k: jax.random.permutation(k, N_INNODE))(jax.random.split(inner_key, blocks * N_NODE)).astype(jnp.int32)
    inner_perm = inner_perm.reshape(blocks, N_NODE * N_INNODE)
    node_final = jnp.take_along_axis(node_perm, node_raw.reshape(blocks, -1), axis=1)
    inner_final = jnp.take_along_axis(inner_perm, (node_raw * N_INNODE + inner_raw).reshape(blocks, -1), axis=1)
    chosen = (node_final * N_INNODE + inner_final).reshape(blocks, TOK_DEV, TOP)
    order = jax.vmap(lambda k: jax.random.permutation(k, TOK_DEV))(jax.random.split(order_key, blocks)).astype(jnp.int32)
    chosen = jnp.take_along_axis(chosen, order[:, :, None], axis=1)
    return chosen.reshape(TOKENS, TOP).astype(jnp.int32)


def shard_levels(key, shape, shards, low, top_value):
    loudness = 1.0
    for dim, shards_of in shards:
        steps = jax.random.uniform(jax.random.fold_in(jax.random.fold_in(key, 6), dim), (shards_of,), jnp.float32, low / len(shards), top_value / len(shards))
        loudness = loudness * jnp.repeat(jnp.exp(steps), shape[dim] // shards_of).reshape((-1,) + (1,) * (len(shape) - 1 - dim))
    return loudness


def gaussian(stream_key, dims, deviation, limit, shards=(), kind=jnp.bfloat16):
    factor_of = shard_levels(stream_key, dims, shards, -0.22, 0.18) if shards else 1.0
    result = jax.random.normal(stream_key, dims, jnp.float32) * deviation * factor_of
    return jnp.minimum(jnp.maximum(result, -limit), limit).astype(kind)


def setup_inputs(seed: int = 0) -> dict:
    key_list = jax.random.split(jax.random.key(seed), 8)
    return {
        "tokens": gaussian(key_list[0], (TOKENS, D), 1.0, 6.0, ((0, 128),)),
        "routes": draw_routes(jax.random.fold_in(key_list[7], 71), 0),
        "route_gates": jnp.clip(0.1 + 0.9 * jax.random.uniform(key_list[2], (TOKENS, TOP), jnp.float32) ** shard_levels(key_list[2], (TOKENS, TOP), ((0, 128),), -0.2, 0.2), 0.1, 1.0),
        "out_grad": gaussian(key_list[3], (TOKENS, D), 0.3, 4.0, ((0, 128),)),
        "gate_weight": gaussian(key_list[4], (EXPERTS, D, W), D ** -0.5, 0.125, ((0, 32), (1, 32))),
        "up_weight": gaussian(key_list[5], (EXPERTS, D, W), D ** -0.5, 0.125, ((0, 32), (1, 32))),
        "down_weight": gaussian(key_list[6], (EXPERTS, D, W), W ** -0.5, 0.21875, ((0, 32), (1, 32))),
    }


def block_slots(block_routes):
    hits = (block_routes[:, None] == jnp.arange(EXPERTS, dtype=jnp.int32)[None, :]).astype(jnp.int32)
    earlier = jnp.cumsum(hits, axis=0) - hits
    return jnp.sum(earlier * hits, axis=1).astype(jnp.int32)


def reference(tokens, routes, route_gates, out_grad, gate_weight, up_weight, down_weight):
    blocks = TOKENS // TOK_DEV
    per_block = routes.reshape(blocks, TOK_DEV * TOP)
    slots = jax.vmap(block_slots)(per_block)
    block_ids = jnp.arange(blocks, dtype=jnp.int32)[:, None]
    position = (block_ids * CAP + slots).reshape(-1).astype(jnp.int32)
    owners = (block_ids * TOK_DEV + jnp.arange(TOK_DEV * TOP, dtype=jnp.int32)[None, :] // TOP).reshape(-1).astype(jnp.int32)
    expert_ids = routes.reshape(-1).astype(jnp.int32)
    table = jnp.full((EXPERTS, blocks * CAP), TOKENS, jnp.int32).at[expert_ids, position].set(owners)
    gate_table = jnp.zeros((EXPERTS, blocks * CAP), jnp.float32).at[expert_ids, position].set(route_gates.reshape(-1))
    padded_tokens = jnp.concatenate([tokens, jnp.zeros((1, D), jnp.bfloat16)], axis=0)
    padded_grad = jnp.concatenate([out_grad, jnp.zeros((1, D), jnp.bfloat16)], axis=0)

    def one_expert(operands):
        index, gates, gate_w, up_w, down_w = operands
        rows_in = padded_tokens[index]
        weighted = (gates[:, None] * padded_grad[index].astype(jnp.float32)).astype(jnp.bfloat16)
        gate_pre = jnp.dot(rows_in, gate_w, preferred_element_type=jnp.float32)
        up_pre = jnp.dot(rows_in, up_w, preferred_element_type=jnp.float32)
        sigma = jax.nn.sigmoid(gate_pre)
        hidden_grad = jnp.dot(weighted, down_w, preferred_element_type=jnp.float32)
        gate_grad = (hidden_grad * up_pre * sigma * (1.0 + gate_pre * (1.0 - sigma))).astype(jnp.bfloat16)
        up_grad = (hidden_grad * gate_pre * sigma).astype(jnp.bfloat16)
        back = (jnp.dot(gate_grad, gate_w.T, preferred_element_type=jnp.float32)
                + jnp.dot(up_grad, up_w.T, preferred_element_type=jnp.float32)).astype(jnp.bfloat16)
        return back

    backs = lax.map(one_expert, (table, gate_table, gate_weight, up_weight, down_weight))
    summed = jnp.zeros((TOKENS + 1, D), jnp.float32).at[table.reshape(-1)].add(backs.reshape(-1, D).astype(jnp.float32))
    return summed[:TOKENS].astype(jnp.bfloat16)
```

```python
import functools

import jax
import jax.numpy as jnp
from jax import lax
from jax.experimental import pallas as pl
from jax.experimental.pallas import tpu as pltpu
from jax.sharding import PartitionSpec as P

MESH = pl.DeviceIdType.MESH
F32 = jnp.float32
BF16 = jnp.bfloat16

CW = 256
ROWS = 24
SLOT = 32
DC = 512


def body(
    nz, nx, ny,
    tok_hbm, routes_hbm, gates_hbm, grad_hbm, gate_hbm, up_hbm, down_hbm,
    out_ref,
    wbuf, tok, grd, rts, gts, xs, xr, lhs, acc, hid, back, ret_out, ret_in, part, yr,
    in_sem, own_sem, z_send, z_recv, p_send, p_recv, x_sem, r_send, r_recv, y_send, y_recv,
):
    half = nz // 2
    n_w = wbuf.shape[0]
    pairs = nz // 2
    n_dc = nz * 128 // DC
    dp = lax.axis_index("dp")
    x = lax.axis_index("node")
    y = lax.axis_index("innode")
    z, c = lax.div(dp, 2), lax.rem(dp, 2)
    nxt = lax.rem(z + 1, nz) * 2 + c
    prv = lax.rem(z + nz - 1, nz) * 2 + c
    ring = ({"dp": nxt}, {"dp": prv})
    partner = {"dp": z * 2 + 1 - c}
    x_to = [{"node": lax.rem(x + r, nx)} for r in range(nx)]
    x_back = [{"node": lax.rem(x + nx - r, nx)} for r in range(nx)]
    y_to = [{"innode": lax.rem(y + i, ny)} for i in range(ny)]

    def mine(ref, w, pos):
        return ref.at[w, :, pos, pl.ds(pl.multiple_of(c * 64, 64), 64), :]

    def mine2(w, s):
        return wbuf.at[w, :, pl.ds(2 * s, 2), pl.ds(pl.multiple_of(c * 64, 64), 64), :]

    def piece(w, pos, sub):
        return wbuf.at[w, :, pos, pl.ds(pl.multiple_of(c * 64 + sub * 32, 32), 32), :]

    own = []
    for w in range(n_w):
        for m, ref in enumerate((gate_hbm, up_hbm, down_hbm)):
            copy = pltpu.make_async_copy(
                ref.at[0, :, pl.ds(w * CW, CW)],
                wbuf.at[w, m, 0, pl.ds(pl.multiple_of(c * 64, 64), 64), :],
                own_sem.at[w, m],
            )
            copy.start()
            own.append(copy)
    ins = []
    for i, (a, b) in enumerate(
        ((routes_hbm, rts), (gates_hbm, gts), (tok_hbm, tok), (grad_hbm, grd))
    ):
        copy = pltpu.make_async_copy(a, b, in_sem.at[i])
        copy.start()
        ins.append(copy)

    barrier = pltpu.get_barrier_semaphore()
    peers = [ring[0], ring[1], partner] + x_to[1:] + y_to[1:]
    for peer in peers:
        pl.semaphore_signal(barrier, inc=1, device_id=peer, device_id_type=MESH)
    pl.semaphore_wait(barrier, len(peers))

    def z_copy(w, s, d, sub, src, dst):
        return pltpu.make_async_remote_copy(
            src_ref=piece(w, src, sub),
            dst_ref=piece(w, dst, sub),
            send_sem=z_send.at[w, s, d, sub],
            recv_sem=z_recv.at[w, s, d, sub],
            device_id=ring[d],
            device_id_type=MESH,
        )

    def p_copy(w, s):
        ref = mine2(w, s) if 0 < s < half else mine(wbuf, w, 0 if s == 0 else 1)
        return pltpu.make_async_remote_copy(
            src_ref=ref,
            dst_ref=ref,
            send_sem=p_send.at[w, s],
            recv_sem=p_recv.at[w, s],
            device_id=partner,
            device_id_type=MESH,
        )

    sent = []

    def start(copy):
        copy.start()
        sent.append(copy)

    def place(s, d):
        return 0 if s == 0 else (1 if s == half else 2 * s + d)

    def service(w, s):
        for sub in range(2):
            for d in range(2):
                if s == half and sub != d:
                    continue
                z_copy(w, s, d, sub, place(s - 1, d), place(s, d)).wait_recv()
                if s + 1 < half or (s + 1 == half and sub == d):
                    start(z_copy(w, s + 1, d, sub, place(s, d), place(s + 1, d)))
        start(p_copy(w, s))

    for w in range(n_w):
        for m in range(3):
            own[w * 3 + m].wait()
        for sub in range(2):
            for d in range(2):
                if half > 1 or sub == d:
                    start(z_copy(w, 1, d, sub, 0, place(1, d)))
    for w in range(n_w):
        start(p_copy(w, 0))

    ins[0].wait()
    ins[1].wait()
    n_tok = rts.shape[1]
    lanes = nx * SLOT
    line = lax.broadcasted_iota(jnp.int32, (lanes, n_tok), 0)
    slot = line & (SLOT - 1)
    group = x + (line >> 5)
    group = jnp.where(group >= nx, group - nx, group)
    expert = group * ny + y
    hit = jnp.zeros((lanes, n_tok), F32)
    weight = jnp.zeros((lanes, n_tok), F32)
    for k in range(rts.shape[0]):
        same = rts[k : k + 1, :] == expert
        hit = jnp.where(same, 1.0, hit)
        weight = jnp.where(same, gts[k : k + 1, :], weight)
    earlier = (
        lax.broadcasted_iota(jnp.int32, (n_tok, n_tok), 0)
        < lax.broadcasted_iota(jnp.int32, (n_tok, n_tok), 1)
    ).astype(F32).astype(BF16)
    rank = jnp.dot(hit.astype(BF16), earlier, preferred_element_type=F32)
    slot1 = jnp.where(slot < 16, slot, jnp.where(slot >= 24, slot - 8, -1))
    own0 = jnp.where(rank == slot.astype(F32), hit, 0.0)
    own1 = jnp.where(rank == slot1.astype(F32), hit, 0.0)
    pick = own0.astype(BF16)
    scale = jnp.sum(own0 * weight, axis=1, keepdims=True)
    spread = (jnp.transpose(own0).astype(BF16), jnp.transpose(own1).astype(BF16))

    ins[2].wait()
    ins[3].wait()
    for p in range(pairs):
        first = pl.multiple_of(lax.rem(z + nz - p, nz) * 128, 128)
        second = pl.multiple_of(lax.rem(z + (half if p == 0 else p), nz) * 128, 128)
        cols = pl.ds(p * 256, 256)
        a = jnp.concatenate([tok[:, pl.ds(first, 128)], tok[:, pl.ds(second, 128)]], axis=1)
        b = jnp.concatenate([grd[:, pl.ds(first, 128)], grd[:, pl.ds(second, 128)]], axis=1)
        a = jnp.dot(pick, a, preferred_element_type=F32)
        b = jnp.dot(pick, b, preferred_element_type=F32) * scale
        for r in range(nx):
            o = r * SLOT
            xs[r, 0:16, cols] = a[o : o + 16].astype(BF16)
            xs[r, 16:32, cols] = b[o : o + 16].astype(BF16)
            xs[r, 32:48, cols] = jnp.concatenate(
                [a[o + 16 : o + 24], b[o + 16 : o + 24]], axis=0
            ).astype(BF16)
    x_copies = []
    for r in range(1, nx):
        copy = pltpu.make_async_remote_copy(
            src_ref=xs.at[r],
            dst_ref=xr.at[r - 1],
            send_sem=x_sem.at[0, r],
            recv_sem=x_sem.at[1, r],
            device_id=x_to[r],
            device_id_type=MESH,
        )
        start(copy)
        x_copies.append(copy)

    def assemble():
        for copy in x_copies:
            copy.wait_recv()
        got = [xs.at[0]] + [xr.at[r - 1] for r in range(1, nx)]
        for r in range(nx):
            lhs[0, r * 16 : r * 16 + 16, :] = got[r][0:16, :]
            lhs[1, r * 16 : r * 16 + 16, :] = got[r][16:32, :]
        for r in range(0, nx, 2):
            a = got[r][32:48, :].astype(F32)
            b = got[r + 1][32:48, :].astype(F32)
            o = nx * 16 + r * 8
            lhs[0, o : o + 16, :] = jnp.concatenate([a[0:8], b[0:8]], axis=0).astype(BF16)
            lhs[1, o : o + 16, :] = jnp.concatenate([a[8:16], b[8:16]], axis=0).astype(BF16)

    def weights(w, m, p):
        return wbuf[w, m, 2 * p : 2 * p + 2].reshape(256, CW)

    def forward(w, p):
        cols = slice(p * 256, p * 256 + 256)
        if p == 0:
            p_copy(w, 0).wait_recv()
            p_copy(w, half).wait_recv()
        else:
            p_copy(w, p).wait_recv()
        for m in range(3):
            term = jnp.dot(
                lhs[m // 2, :, cols], weights(w, m, p), preferred_element_type=F32
            )
            if p == 1 or pairs == 1:
                acc[m] = term
            else:
                acc[m] += term

    def middle(w):
        gate_pre, up_pre, hidden = acc[0], acc[1], acc[2]
        sigma = 1.0 / (1.0 + jnp.exp(-gate_pre))
        hid[0] = (hidden * up_pre * sigma * (1.0 + gate_pre * (1.0 - sigma))).astype(BF16)
        hid[1] = (hidden * gate_pre * sigma).astype(BF16)

    over = (((1,), (1,)), ((), ()))

    def backward(w, p):
        cols = slice(p * 256, p * 256 + 256)
        term = lax.dot_general(hid[0], weights(w, 0, p), over, preferred_element_type=F32)
        term += lax.dot_general(hid[1], weights(w, 1, p), over, preferred_element_type=F32)
        if w == 0:
            back[:, cols] = term
        elif w + 1 < n_w:
            back[:, cols] += term
        else:
            return back[:, cols] + term

    steps = [(0, s) for s in range(1, half)]
    for w in range(n_w):
        if w + 1 < n_w:
            steps += [(w + 1, 1), (w, half)] if half > 1 else [(w, half), (w + 1, 1)]
            steps += [(w + 1, s) for s in range(2, half)]
        else:
            steps += [(w, half)]
    seen, steps2 = set(), []
    for step in steps:
        if step not in seen:
            seen.add(step)
            steps2.append(step)
    order = list(range(1, pairs)) + [0]
    queue = [(0, None, assemble)]
    for w in range(n_w):
        for p in order:
            queue.append((3, (w, p if p else half), functools.partial(forward, w, p)))
        queue.append((2, None, functools.partial(middle, w)))
        if w + 1 < n_w:
            for p in order:
                queue.append((2, None, functools.partial(backward, w, p)))
    done = set()
    for i, step in enumerate(steps2):
        service(*step)
        if i >= min(5, half - 1):
            budget = 10
            while queue and budget > 0 and (queue[0][1] is None or queue[0][1] in done):
                cost, _, work = queue.pop(0)
                work()
                budget -= cost
        done.add(step)
    for _, _, work in queue:
        work()

    last = n_w - 1
    ret = []
    for dc in range(n_dc):
        a, b = backward(last, 2 * dc), backward(last, 2 * dc + 1)
        for r in range(nx):
            o, q = r * 16, nx * 16 + r * 8
            dest = ret_in.at[dc, 0] if r == 0 else ret_out.at[dc, r - 1]
            dest[0:16, :] = a[o : o + 16].astype(BF16)
            dest[16:32, :] = b[o : o + 16].astype(BF16)
            dest[32:48, :] = jnp.concatenate([a[q : q + 8], b[q : q + 8]], axis=0).astype(BF16)
        ret.append([])
        for r in range(1, nx):
            copy = pltpu.make_async_remote_copy(
                src_ref=ret_out.at[dc, r - 1],
                dst_ref=ret_in.at[dc, r],
                send_sem=r_send.at[dc, r],
                recv_sem=r_recv.at[dc, r],
                device_id=x_back[r],
                device_id_type=MESH,
            )
            start(copy)
            ret[-1].append(copy)
    y_copies = []
    for dc in range(n_dc):
        for copy in ret[dc]:
            copy.wait_recv()
        for h in range(2):
            rows = []
            for r in range(nx):
                rows += [ret_in[dc, r, h * 16 : h * 16 + 16, :], ret_in[dc, r, 32:48, :]]
            part[dc, :, h * 256 : h * 256 + 256] = jnp.dot(
                spread[h], jnp.concatenate(rows, axis=0), preferred_element_type=F32
            ).astype(BF16)
        y_copies.append([])
        for i in range(1, ny):
            to = pl.multiple_of(lax.rem(y + i, ny) * 16, 16)
            copy = pltpu.make_async_remote_copy(
                src_ref=part.at[dc, pl.ds(to, 16), :],
                dst_ref=yr.at[dc, i - 1],
                send_sem=y_send.at[dc, i],
                recv_sem=y_recv.at[dc, i],
                device_id=y_to[i],
                device_id_type=MESH,
            )
            start(copy)
            y_copies[-1].append(copy)
    for dc in range(n_dc):
        total = part[dc, pl.ds(pl.multiple_of(y * 16, 16), 16), :].astype(F32)
        for i in range(1, ny):
            y_copies[dc][i - 1].wait_recv()
            total += yr[dc, i - 1].astype(F32)
        total = total.astype(BF16)
        for i in range(DC // 128):
            pos = dc * (DC // 128) + i
            p = pos // 2
            if pos % 2 == 0:
                src = lax.rem(z + nz - p, nz)
            else:
                src = lax.rem(z + (half if p == 0 else p), nz)
            out_ref[:, pl.ds(pl.multiple_of(src * 128, 128), 128)] = total[
                :, i * 128 : i * 128 + 128
            ]
    for copy in sent:
        copy.wait_send()


def solution(mesh):
    nz, nx, ny = mesh.shape["dp"] // 2, mesh.shape["node"], mesh.shape["innode"]

    def local(tokens, routes, route_gates, out_grad, gate_weight, up_weight, down_weight):
        n_tok, width = tokens.shape
        n_w = gate_weight.shape[2] // CW
        rows = nx * ROWS
        n_dc = width // DC
        half = nz // 2
        any_space = pl.BlockSpec(memory_space=pl.ANY)
        dma = pltpu.SemaphoreType.DMA
        return pl.pallas_call(
            functools.partial(body, nz, nx, ny),
            out_shape=jax.ShapeDtypeStruct((n_tok // ny, width), BF16),
            in_specs=[any_space] * 7,
            out_specs=pl.BlockSpec(memory_space=pltpu.VMEM),
            scratch_shapes=[
                pltpu.VMEM((n_w, 3, nz, 128, CW), BF16),
                pltpu.VMEM((n_tok, width), BF16),
                pltpu.VMEM((n_tok, width), BF16),
                pltpu.VMEM(routes.shape[::-1], jnp.int32),
                pltpu.VMEM(route_gates.shape[::-1], F32),
                pltpu.VMEM((nx, 48, width), BF16),
                pltpu.VMEM((nx - 1, 48, width), BF16),
                pltpu.VMEM((2, rows, width), BF16),
                pltpu.VMEM((3, rows, CW), F32),
                pltpu.VMEM((2, rows, CW), BF16),
                pltpu.VMEM((rows, width), F32),
                pltpu.VMEM((n_dc, nx - 1, 48, 256), BF16),
                pltpu.VMEM((n_dc, nx, 48, 256), BF16),
                pltpu.VMEM((n_dc, n_tok, DC), BF16),
                pltpu.VMEM((n_dc, max(ny - 1, 1), n_tok // ny, DC), BF16),
                dma((4,)),
                dma((n_w, 3)),
                dma((n_w, half + 1, 2, 2)),
                dma((n_w, half + 1, 2, 2)),
                dma((n_w, half + 1)),
                dma((n_w, half + 1)),
                dma((2, nx)),
                dma((n_dc, nx)),
                dma((n_dc, nx)),
                dma((n_dc, ny)),
                dma((n_dc, ny)),
            ],
            compiler_params=pltpu.CompilerParams(
                collective_id=0, has_side_effects=True, vmem_limit_bytes=60 * 1024 * 1024
            ),
            cost_estimate=pl.CostEstimate(
                flops=10 * rows * width * gate_weight.shape[2],
                bytes_accessed=16 * 1024 * 1024,
                transcendentals=rows * gate_weight.shape[2],
            ),
            name="moe_input_grad",
        )(tokens, routes.T, route_gates.T, out_grad, gate_weight, up_weight, down_weight)

    return jax.shard_map(
        local,
        mesh=mesh,
        in_specs=(
            P(("dp", "node"), None),
            P(("dp", "node"), None),
            P(("dp", "node"), None),
            P(("dp", "node"), None),
            P(("node", "innode"), "dp", None),
            P(("node", "innode"), "dp", None),
            P(("node", "innode"), "dp", None),
        ),
        out_specs=P(("dp", "node", "innode"), None),
        check_vma=False,
    )
```

```python
import functools

import jax
import jax.numpy as jnp
from jax import lax
from jax.experimental import pallas as pl
from jax.experimental.pallas import tpu as pltpu
from jax.sharding import PartitionSpec as P

MESH = pl.DeviceIdType.MESH
F32 = jnp.float32
BF16 = jnp.bfloat16

ROWS = 24
SLOT = 32
DC = 512


def body(
    nz, nx, ny,
    tok_hbm, routes_hbm, gates_hbm, grad_hbm, gate_hbm, up_hbm, down_hbm,
    out_ref,
    wbuf, tok, grd, rts, gts, xs, xr, lhs, acc, hid, ret_out, ret_in, part, yr,
    in_sem, own_sem, z_send, z_recv, p_send, p_recv, x_sem, r_send, r_recv, y_send, y_recv,
):
    half = nz // 2
    pairs = nz // 2
    n_dc = nz * 128 // DC
    dp = lax.axis_index("dp")
    x = lax.axis_index("node")
    y = lax.axis_index("innode")
    z, c = lax.div(dp, 2), lax.rem(dp, 2)
    nxt = lax.rem(z + 1, nz) * 2 + c
    prv = lax.rem(z + nz - 1, nz) * 2 + c
    ring = ({"dp": nxt}, {"dp": prv})
    partner = {"dp": z * 2 + 1 - c}
    x_to = [{"node": lax.rem(x + r, nx)} for r in range(nx)]
    x_back = [{"node": lax.rem(x + nx - r, nx)} for r in range(nx)]
    y_to = [{"innode": lax.rem(y + i, ny)} for i in range(ny)]

    def mine(m, pos, count):
        return wbuf.at[m, pl.ds(pos, count), pl.ds(pl.multiple_of(c * 64, 64), 64), :]

    def piece(m, pos, s, d):
        if s == half:
            return wbuf.at[m, pos, pl.ds(pl.multiple_of(c * 64 + d * 32, 32), 32), :]
        return wbuf.at[m, pos, pl.ds(pl.multiple_of(c * 64, 64), 64), :]

    own = []
    for m, ref in enumerate((gate_hbm, up_hbm, down_hbm)):
        copy = pltpu.make_async_copy(ref, mine(m, 0, 1), own_sem.at[m])
        copy.start()
        own.append(copy)
    ins = []
    for i, (a, b) in enumerate(
        ((routes_hbm, rts), (gates_hbm, gts), (tok_hbm, tok), (grad_hbm, grd))
    ):
        copy = pltpu.make_async_copy(a, b, in_sem.at[i])
        copy.start()
        ins.append(copy)

    barrier = pltpu.get_barrier_semaphore()
    peers = [ring[0], ring[1], partner] + x_to[1:] + y_to[1:]
    for peer in peers:
        pl.semaphore_signal(barrier, inc=1, device_id=peer, device_id_type=MESH)
    pl.semaphore_wait(barrier, len(peers))

    def z_copy(s, m, d):
        return pltpu.make_async_remote_copy(
            src_ref=piece(m, place(s - 1, d), s, d),
            dst_ref=piece(m, place(s, d), s, d),
            send_sem=z_send.at[s, m, d],
            recv_sem=z_recv.at[s, m, d],
            device_id=ring[d],
            device_id_type=MESH,
        )

    def p_copy(s, m):
        ref = mine(m, 2 * s, 2) if 0 < s < half else mine(m, 0 if s == 0 else 1, 1)
        return pltpu.make_async_remote_copy(
            src_ref=ref,
            dst_ref=ref,
            send_sem=p_send.at[s, m],
            recv_sem=p_recv.at[s, m],
            device_id=partner,
            device_id_type=MESH,
        )

    sent = []

    def start(copy):
        copy.start()
        sent.append(copy)

    def place(s, d):
        return 0 if s == 0 else (1 if s == half else 2 * s + d)

    def service(s):
        for m in range(3):
            for d in range(2):
                z_copy(s, m, d).wait_recv()
                if s < half:
                    start(z_copy(s + 1, m, d))
            start(p_copy(s, m))

    for m in range(3):
        own[m].wait()
        for d in range(2):
            start(z_copy(1, m, d))
    for m in range(3):
        start(p_copy(0, m))

    ins[0].wait()
    ins[1].wait()
    n_tok = rts.shape[1]
    lanes = nx * SLOT
    line = lax.broadcasted_iota(jnp.int32, (lanes, n_tok), 0)
    slot = line & (SLOT - 1)
    group = x + (line >> 5)
    group = jnp.where(group >= nx, group - nx, group)
    expert = group * ny + y
    hit = jnp.zeros((lanes, n_tok), F32)
    weight = jnp.zeros((lanes, n_tok), F32)
    for k in range(rts.shape[0]):
        same = rts[k : k + 1, :] == expert
        hit = jnp.where(same, 1.0, hit)
        weight = jnp.where(same, gts[k : k + 1, :], weight)
    earlier = (
        lax.broadcasted_iota(jnp.int32, (n_tok, n_tok), 0)
        < lax.broadcasted_iota(jnp.int32, (n_tok, n_tok), 1)
    ).astype(F32).astype(BF16)
    rank = jnp.dot(hit.astype(BF16), earlier, preferred_element_type=F32)
    slot1 = jnp.where(slot < 16, slot, jnp.where(slot >= 24, slot - 8, -1))
    own0 = jnp.where(rank == slot.astype(F32), hit, 0.0)
    own1 = jnp.where(rank == slot1.astype(F32), hit, 0.0)
    pick = own0.astype(BF16)
    scale = jnp.sum(own0 * weight, axis=1, keepdims=True)
    spread = (jnp.transpose(own0).astype(BF16), jnp.transpose(own1).astype(BF16))

    ins[2].wait()
    ins[3].wait()
    for p in range(pairs):
        first = pl.multiple_of(lax.rem(z + nz - p, nz) * 128, 128)
        second = pl.multiple_of(lax.rem(z + (half if p == 0 else p), nz) * 128, 128)
        cols = pl.ds(p * 256, 256)
        a = jnp.concatenate([tok[:, pl.ds(first, 128)], tok[:, pl.ds(second, 128)]], axis=1)
        b = jnp.concatenate([grd[:, pl.ds(first, 128)], grd[:, pl.ds(second, 128)]], axis=1)
        a = jnp.dot(pick, a, preferred_element_type=F32)
        b = jnp.dot(pick, b, preferred_element_type=F32) * scale
        for r in range(nx):
            o = r * SLOT
            xs[r, 0:16, cols] = a[o : o + 16].astype(BF16)
            xs[r, 16:32, cols] = b[o : o + 16].astype(BF16)
            xs[r, 32:48, cols] = jnp.concatenate(
                [a[o + 16 : o + 24], b[o + 16 : o + 24]], axis=0
            ).astype(BF16)
    x_copies = []
    for r in range(1, nx):
        copy = pltpu.make_async_remote_copy(
            src_ref=xs.at[r],
            dst_ref=xr.at[r - 1],
            send_sem=x_sem.at[0, r],
            recv_sem=x_sem.at[1, r],
            device_id=x_to[r],
            device_id_type=MESH,
        )
        start(copy)
        x_copies.append(copy)

    def assemble():
        for copy in x_copies:
            copy.wait_recv()
        got = [xs.at[0]] + [xr.at[r - 1] for r in range(1, nx)]
        for r in range(nx):
            lhs[0, r * 16 : r * 16 + 16, :] = got[r][0:16, :]
            lhs[1, r * 16 : r * 16 + 16, :] = got[r][16:32, :]
        for r in range(0, nx, 2):
            a = got[r][32:48, :].astype(F32)
            b = got[r + 1][32:48, :].astype(F32)
            o = nx * 16 + r * 8
            lhs[0, o : o + 16, :] = jnp.concatenate([a[0:8], b[0:8]], axis=0).astype(BF16)
            lhs[1, o : o + 16, :] = jnp.concatenate([a[8:16], b[8:16]], axis=0).astype(BF16)

    def forward(p, m):
        if p == 0:
            p_copy(0, m).wait_recv()
            p_copy(half, m).wait_recv()
        else:
            p_copy(p, m).wait_recv()
        width = wbuf.shape[3]
        term = jnp.dot(
            lhs[m // 2, :, p * 256 : p * 256 + 256],
            wbuf[m, 2 * p : 2 * p + 2].reshape(256, width),
            preferred_element_type=F32,
        )
        if p == (1 if pairs > 1 else 0):
            acc[m] = term
        else:
            acc[m] += term

    wait_steps = min(3, half - 1)
    ready = []
    for s in range(1, half):
        service(s)
        if s == wait_steps:
            assemble()
        if s >= wait_steps:
            while ready:
                p = ready.pop(0)
                for m in range(3):
                    forward(p, m)
        ready.append(s)
    for p in ready:
        for m in range(3):
            forward(p, m)
    service(half)
    for m in range(3):
        forward(0, m)
    gate_pre, up_pre, hidden = acc[0], acc[1], acc[2]
    sigma = 1.0 / (1.0 + jnp.exp(-gate_pre))
    hid[0] = (hidden * up_pre * sigma * (1.0 + gate_pre * (1.0 - sigma))).astype(BF16)
    hid[1] = (hidden * gate_pre * sigma).astype(BF16)

    over = (((1,), (1,)), ((), ()))

    def backward(p):
        term = None
        for m in range(2):
            rhs = wbuf[m, 2 * p : 2 * p + 2].reshape(256, wbuf.shape[3])
            part_sum = lax.dot_general(hid[m], rhs, over, preferred_element_type=F32)
            term = part_sum if term is None else term + part_sum
        return term

    ret = []
    for dc in range(n_dc):
        a, b = backward(2 * dc), backward(2 * dc + 1)
        for r in range(nx):
            o, q = r * 16, nx * 16 + r * 8
            dest = ret_in.at[dc, 0] if r == 0 else ret_out.at[dc, r - 1]
            dest[0:16, :] = a[o : o + 16].astype(BF16)
            dest[16:32, :] = b[o : o + 16].astype(BF16)
            dest[32:48, :] = jnp.concatenate([a[q : q + 8], b[q : q + 8]], axis=0).astype(BF16)
        ret.append([])
        for r in range(1, nx):
            copy = pltpu.make_async_remote_copy(
                src_ref=ret_out.at[dc, r - 1],
                dst_ref=ret_in.at[dc, r],
                send_sem=r_send.at[dc, r],
                recv_sem=r_recv.at[dc, r],
                device_id=x_back[r],
                device_id_type=MESH,
            )
            start(copy)
            ret[-1].append(copy)
    y_copies = []
    for dc in range(n_dc):
        for copy in ret[dc]:
            copy.wait_recv()
        for h in range(2):
            rows = []
            for r in range(nx):
                rows += [ret_in[dc, r, h * 16 : h * 16 + 16, :], ret_in[dc, r, 32:48, :]]
            part[dc, :, h * 256 : h * 256 + 256] = jnp.dot(
                spread[h], jnp.concatenate(rows, axis=0), preferred_element_type=F32
            ).astype(BF16)
        y_copies.append([])
        for i in range(1, ny):
            to = pl.multiple_of(lax.rem(y + i, ny) * 16, 16)
            copy = pltpu.make_async_remote_copy(
                src_ref=part.at[dc, pl.ds(to, 16), :],
                dst_ref=yr.at[dc, i - 1],
                send_sem=y_send.at[dc, i],
                recv_sem=y_recv.at[dc, i],
                device_id=y_to[i],
                device_id_type=MESH,
            )
            start(copy)
            y_copies[-1].append(copy)
    for dc in range(n_dc):
        total = part[dc, pl.ds(pl.multiple_of(y * 16, 16), 16), :].astype(F32)
        for i in range(1, ny):
            y_copies[dc][i - 1].wait_recv()
            total += yr[dc, i - 1].astype(F32)
        total = total.astype(BF16)
        for i in range(DC // 128):
            pos = dc * (DC // 128) + i
            p = pos // 2
            if pos % 2 == 0:
                src = lax.rem(z + nz - p, nz)
            else:
                src = lax.rem(z + (half if p == 0 else p), nz)
            out_ref[:, pl.ds(pl.multiple_of(src * 128, 128), 128)] = total[
                :, i * 128 : i * 128 + 128
            ]
    for copy in sent:
        copy.wait_send()


def solution(mesh):
    nz, nx, ny = mesh.shape["dp"] // 2, mesh.shape["node"], mesh.shape["innode"]

    def local(tokens, routes, route_gates, out_grad, gate_weight, up_weight, down_weight):
        n_tok, width = tokens.shape
        units = gate_weight.shape[2]
        rows = nx * ROWS
        n_dc = width // DC
        half = nz // 2
        any_space = pl.BlockSpec(memory_space=pl.ANY)
        dma = pltpu.SemaphoreType.DMA
        return pl.pallas_call(
            functools.partial(body, nz, nx, ny),
            out_shape=jax.ShapeDtypeStruct((n_tok // ny, width), BF16),
            in_specs=[any_space] * 7,
            out_specs=pl.BlockSpec(memory_space=pltpu.VMEM),
            scratch_shapes=[
                pltpu.VMEM((3, nz, 128, units), BF16),
                pltpu.VMEM((n_tok, width), BF16),
                pltpu.VMEM((n_tok, width), BF16),
                pltpu.VMEM(routes.shape[::-1], jnp.int32),
                pltpu.VMEM(route_gates.shape[::-1], F32),
                pltpu.VMEM((nx, 48, width), BF16),
                pltpu.VMEM((nx - 1, 48, width), BF16),
                pltpu.VMEM((2, rows, width), BF16),
                pltpu.VMEM((3, rows, units), F32),
                pltpu.VMEM((2, rows, units), BF16),
                pltpu.VMEM((n_dc, nx - 1, 48, 256), BF16),
                pltpu.VMEM((n_dc, nx, 48, 256), BF16),
                pltpu.VMEM((n_dc, n_tok, DC), BF16),
                pltpu.VMEM((n_dc, max(ny - 1, 1), n_tok // ny, DC), BF16),
                dma((4,)),
                dma((3,)),
                dma((half + 1, 3, 2)),
                dma((half + 1, 3, 2)),
                dma((half + 1, 3)),
                dma((half + 1, 3)),
                dma((2, nx)),
                dma((n_dc, nx)),
                dma((n_dc, nx)),
                dma((n_dc, ny)),
                dma((n_dc, ny)),
            ],
            compiler_params=pltpu.CompilerParams(
                collective_id=0, has_side_effects=True, vmem_limit_bytes=60 * 1024 * 1024
            ),
            cost_estimate=pl.CostEstimate(
                flops=10 * rows * width * units,
                bytes_accessed=16 * 1024 * 1024,
                transcendentals=rows * units,
            ),
            name="moe_input_grad",
        )(tokens, routes.T, route_gates.T, out_grad, gate_weight, up_weight, down_weight)

    return jax.shard_map(
        local,
        mesh=mesh,
        in_specs=(
            P(("dp", "node"), None),
            P(("dp", "node"), None),
            P(("dp", "node"), None),
            P(("dp", "node"), None),
            P(("node", "innode"), "dp", None),
            P(("node", "innode"), "dp", None),
            P(("node", "innode"), "dp", None),
        ),
        out_specs=P(("dp", "node", "innode"), None),
        check_vma=False,
    )
```

```python
import functools

import jax
import jax.numpy as jnp
from jax import lax
from jax.experimental import pallas as pl
from jax.experimental.pallas import tpu as pltpu
from jax.sharding import PartitionSpec as P

MESH = pl.DeviceIdType.MESH
F32 = jnp.float32
BF16 = jnp.bfloat16

ROWS = 24
SLOT = 32
DC = 1024
HC = DC // 2
LAGS = (0, 1, 2, 3)


def body(
    nz, nx, ny,
    tok_hbm, routes_hbm, gates_hbm, grad_hbm, gate_hbm, up_hbm, down_hbm,
    out_ref,
    wbuf, tok, grd, rts, gts, xs, xr, lhs, acc, hid, ret_out, ret_in, part, y_one, y_side, y_sum, yr,
    in_sem, own_sem, z_send, z_recv, p_send, p_recv, x_sem, r_send, r_recv, y_send, y_recv,
):
    half = nz // 2
    pairs = nz // 2
    n_dc = nz * 128 // DC
    dp = lax.axis_index("dp")
    x = lax.axis_index("node")
    y = lax.axis_index("innode")
    z, c = lax.div(dp, 2), lax.rem(dp, 2)
    nxt = lax.rem(z + 1, nz) * 2 + c
    prv = lax.rem(z + nz - 1, nz) * 2 + c
    ring = ({"dp": nxt}, {"dp": prv})
    partner = {"dp": z * 2 + 1 - c}
    x_to = [{"node": lax.rem(x + r, nx)} for r in range(nx)]
    x_back = [{"node": lax.rem(x + nx - r, nx)} for r in range(nx)]
    y_to = [{"innode": lax.rem(y + i, ny)} for i in range(ny)]

    def mine(m, pos, count):
        return wbuf.at[m, pl.ds(pos, count), pl.ds(pl.multiple_of(c * 64, 64), 64), :]

    def piece(m, pos, s, d):
        if s == half:
            return wbuf.at[m, pos, pl.ds(pl.multiple_of(c * 64 + d * 32, 32), 32), :]
        return wbuf.at[m, pos, pl.ds(pl.multiple_of(c * 64, 64), 64), :]

    own = []
    for m, ref in enumerate((gate_hbm, up_hbm, down_hbm)):
        copy = pltpu.make_async_copy(ref, mine(m, 0, 1), own_sem.at[m])
        copy.start()
        own.append(copy)
    ins = []
    for i, (a, b) in enumerate(
        ((routes_hbm, rts), (gates_hbm, gts), (tok_hbm, tok), (grad_hbm, grd))
    ):
        copy = pltpu.make_async_copy(a, b, in_sem.at[i])
        copy.start()
        ins.append(copy)

    barrier = pltpu.get_barrier_semaphore()
    peers = [ring[0], ring[1], partner] + x_to[1:] + y_to[1:]
    for peer in peers:
        pl.semaphore_signal(barrier, inc=1, device_id=peer, device_id_type=MESH)
    pl.semaphore_wait(barrier, len(peers))

    def z_copy(s, m, d):
        return pltpu.make_async_remote_copy(
            src_ref=piece(m, place(s - 1, d), s, d),
            dst_ref=piece(m, place(s, d), s, d),
            send_sem=z_send.at[s, m, d],
            recv_sem=z_recv.at[s, m, d],
            device_id=ring[d],
            device_id_type=MESH,
        )

    def p_copy(s, m):
        ref = mine(m, 2 * s, 2) if 0 < s < half else mine(m, 0 if s == 0 else 1, 1)
        return pltpu.make_async_remote_copy(
            src_ref=ref,
            dst_ref=ref,
            send_sem=p_send.at[s, m],
            recv_sem=p_recv.at[s, m],
            device_id=partner,
            device_id_type=MESH,
        )

    sent = []

    def start(copy):
        copy.start()
        sent.append(copy)

    def place(s, d):
        return 0 if s == 0 else (1 if s == half else 2 * s + d)

    def service(s):
        for m in range(3):
            for d in range(2):
                z_copy(s, m, d).wait_recv()
                if s < half:
                    start(z_copy(s + 1, m, d))
            start(p_copy(s, m))

    for m in range(3):
        own[m].wait()
        for d in range(2):
            start(z_copy(1, m, d))
    for m in range(3):
        start(p_copy(0, m))

    ins[0].wait()
    ins[1].wait()
    n_tok = rts.shape[1]
    lanes = nx * SLOT
    line = lax.broadcasted_iota(jnp.int32, (lanes, n_tok), 0)
    slot = line & (SLOT - 1)
    group = x + (line >> 5)
    group = jnp.where(group >= nx, group - nx, group)
    expert = group * ny + y
    hit = jnp.zeros((lanes, n_tok), F32)
    weight = jnp.zeros((lanes, n_tok), F32)
    for k in range(rts.shape[0]):
        same = rts[k : k + 1, :] == expert
        hit = jnp.where(same, 1.0, hit)
        weight = jnp.where(same, gts[k : k + 1, :], weight)
    earlier = (
        lax.broadcasted_iota(jnp.int32, (n_tok, n_tok), 0)
        < lax.broadcasted_iota(jnp.int32, (n_tok, n_tok), 1)
    ).astype(F32).astype(BF16)
    rank = jnp.dot(hit.astype(BF16), earlier, preferred_element_type=F32)
    slot1 = jnp.where(slot < 16, slot, jnp.where(slot >= 24, slot - 8, -1))
    own0 = jnp.where(rank == slot.astype(F32), hit, 0.0)
    own1 = jnp.where(rank == slot1.astype(F32), hit, 0.0)
    pick = own0.astype(BF16)
    scale = jnp.sum(own0 * weight, axis=1, keepdims=True)
    spread = (jnp.transpose(own0).astype(BF16), jnp.transpose(own1).astype(BF16))

    ins[2].wait()
    ins[3].wait()
    for p in range(pairs):
        first = pl.multiple_of(lax.rem(z + nz - p, nz) * 128, 128)
        second = pl.multiple_of(lax.rem(z + (half if p == 0 else p), nz) * 128, 128)
        cols = pl.ds(p * 256, 256)
        a = jnp.concatenate([tok[:, pl.ds(first, 128)], tok[:, pl.ds(second, 128)]], axis=1)
        b = jnp.concatenate([grd[:, pl.ds(first, 128)], grd[:, pl.ds(second, 128)]], axis=1)
        a = jnp.dot(pick, a, preferred_element_type=F32)
        b = jnp.dot(pick, b, preferred_element_type=F32) * scale
        for r in range(nx):
            o = r * SLOT
            xs[r, 0:16, cols] = a[o : o + 16].astype(BF16)
            xs[r, 16:32, cols] = b[o : o + 16].astype(BF16)
            xs[r, 32:48, cols] = jnp.concatenate(
                [a[o + 16 : o + 24], b[o + 16 : o + 24]], axis=0
            ).astype(BF16)
    x_copies = []
    for r in range(1, nx):
        copy = pltpu.make_async_remote_copy(
            src_ref=xs.at[r],
            dst_ref=xr.at[r - 1],
            send_sem=x_sem.at[0, r],
            recv_sem=x_sem.at[1, r],
            device_id=x_to[r],
            device_id_type=MESH,
        )
        start(copy)
        x_copies.append(copy)

    def assemble():
        for copy in x_copies:
            copy.wait_recv()
        got = [xs.at[0]] + [xr.at[r - 1] for r in range(1, nx)]
        for r in range(nx):
            lhs[0, r * 16 : r * 16 + 16, :] = got[r][0:16, :]
            lhs[1, r * 16 : r * 16 + 16, :] = got[r][16:32, :]
        for r in range(0, nx, 2):
            a = got[r][32:48, :].astype(F32)
            b = got[r + 1][32:48, :].astype(F32)
            o = nx * 16 + r * 8
            lhs[0, o : o + 16, :] = jnp.concatenate([a[0:8], b[0:8]], axis=0).astype(BF16)
            lhs[1, o : o + 16, :] = jnp.concatenate([a[8:16], b[8:16]], axis=0).astype(BF16)

    def forward(p, m):
        if p == 0:
            p_copy(0, m).wait_recv()
            p_copy(half, m).wait_recv()
        else:
            p_copy(p, m).wait_recv()
        width = wbuf.shape[3]
        term = jnp.dot(
            lhs[m // 2, :, p * 256 : p * 256 + 256],
            wbuf[m, 2 * p : 2 * p + 2].reshape(256, width),
            preferred_element_type=F32,
        )
        if p == (1 if pairs > 1 else 0):
            acc[m] = term
        else:
            acc[m] += term

    wait_steps = min(3, half - 1)
    ready = []
    for s in range(1, half):
        service(s)
        if s == wait_steps:
            assemble()
        if s >= wait_steps:
            while ready:
                p = ready.pop(0)
                for m in range(3):
                    forward(p, m)
        ready.append(s)
    for p in ready:
        for m in range(3):
            forward(p, m)
    service(half)
    forward(0, 0)
    forward(0, 1)
    gate_pre, up_pre = acc[0], acc[1]
    sigma = 1.0 / (1.0 + jnp.exp(-gate_pre))
    acc[0] = up_pre * sigma * (1.0 + gate_pre * (1.0 - sigma))
    acc[1] = gate_pre * sigma
    forward(0, 2)
    hidden = acc[2]
    hid[0] = (hidden * acc[0]).astype(BF16)
    hid[1] = (hidden * acc[1]).astype(BF16)

    over = (((1,), (1,)), ((), ()))

    def backward(p):
        term = None
        for m in range(2):
            rhs = wbuf[m, 2 * p : 2 * p + 2].reshape(256, wbuf.shape[3])
            part_sum = lax.dot_general(hid[m], rhs, over, preferred_element_type=F32)
            term = part_sum if term is None else term + part_sum
        return term

    def r_copy(dc, r):
        return pltpu.make_async_remote_copy(
            src_ref=ret_out.at[dc, r - 1],
            dst_ref=ret_in.at[dc, r],
            send_sem=r_send.at[dc, r],
            recv_sem=r_recv.at[dc, r],
            device_id=x_back[r],
            device_id_type=MESH,
        )

    def send_back(dc):
        a = [backward(dc * (DC // 256) + i) for i in range(DC // 256)]
        a = a[0] if len(a) == 1 else jnp.concatenate(a, axis=1)
        for r in range(nx):
            o, q = r * 16, nx * 16 + r * 8
            dest = ret_in.at[dc, 0] if r == 0 else ret_out.at[dc, r - 1]
            dest[0:16, :] = a[o : o + 16, 0:HC].astype(BF16)
            dest[16:32, :] = a[o : o + 16, HC:DC].astype(BF16)
            dest[32:48, :] = jnp.concatenate(
                [a[q : q + 8, 0:HC], a[q : q + 8, HC:DC]], axis=0
            ).astype(BF16)
            if r:
                start(r_copy(dc, r))

    def rows_of(step):
        return pl.ds(pl.multiple_of(lax.rem(y + step, ny) * 16, 16), 16)

    def y_copy(dc, i):
        src, dst, step = (
            lambda: (part.at[dc, rows_of(ny - 3), :], y_one.at[dc, 0], ny - 1),
            lambda: (part.at[dc, rows_of(3), :], y_one.at[dc, 1], 1),
            lambda: (part.at[dc, rows_of(4), pl.ds(0, HC)], y_side.at[dc, 0], ny - 2),
            lambda: (part.at[dc, rows_of(4), pl.ds(HC, HC)], y_side.at[dc, 1], 2),
            lambda: (part.at[dc, rows_of(ny - 1), :], yr.at[dc, 0], ny - 1),
            lambda: (part.at[dc, rows_of(1), :], yr.at[dc, 1], 1),
            lambda: (y_sum.at[dc, 0], yr.at[dc, 2], ny - 2),
            lambda: (y_sum.at[dc, 1], yr.at[dc, 3], 2),
        )[i]()
        return pltpu.make_async_remote_copy(
            src_ref=src,
            dst_ref=dst,
            send_sem=y_send.at[dc, i],
            recv_sem=y_recv.at[dc, i],
            device_id=y_to[step],
            device_id_type=MESH,
        )

    def add_groups(dc):
        for r in range(1, nx):
            r_copy(dc, r).wait_recv()
        for h in range(2):
            rows = []
            for r in range(nx):
                rows += [ret_in[dc, r, h * 16 : h * 16 + 16, :], ret_in[dc, r, 32:48, :]]
            part[dc, :, h * HC : h * HC + HC] = jnp.dot(
                spread[h], jnp.concatenate(rows, axis=0), preferred_element_type=F32
            ).astype(BF16)
        for i in range(6):
            start(y_copy(dc, i))

    def pass_on(dc):
        for side, step in enumerate((ny - 2, 2)):
            y_copy(dc, side).wait_recv()
            y_copy(dc, 2 + side).wait_recv()
            total = part[dc, rows_of(step), :].astype(F32) + y_one[dc, side].astype(F32)
            cols = slice(side * HC, side * HC + HC)
            far = total[:, cols] + y_side[dc, side].astype(F32)
            near = total[:, HC - side * HC : DC - side * HC]
            y_sum[dc, side, :, cols] = far.astype(BF16)
            y_sum[dc, side, :, HC - side * HC : DC - side * HC] = near.astype(BF16)
            start(y_copy(dc, 6 + side))

    def finish(dc):
        total = part[dc, rows_of(0), :].astype(F32)
        for i in range(4):
            y_copy(dc, 4 + i).wait_recv()
            total += yr[dc, i].astype(F32)
        total = total.astype(BF16)
        for i in range(DC // 128):
            p = (dc * (DC // 128) + i) // 2
            src = z + (half if p == 0 else p) if i % 2 else z + nz - p
            cols = pl.ds(pl.multiple_of(lax.rem(src, nz) * 128, 128), 128)
            out_ref[:, cols] = total[:, i * 128 : i * 128 + 128]

    for t in range(n_dc + LAGS[3]):
        for stage, lag in zip((send_back, add_groups, pass_on, finish), LAGS):
            if 0 <= t - lag < n_dc:
                stage(t - lag)
    for copy in sent:
        copy.wait_send()


def solution(mesh):
    nz, nx, ny = mesh.shape["dp"] // 2, mesh.shape["node"], mesh.shape["innode"]

    def local(tokens, routes, route_gates, out_grad, gate_weight, up_weight, down_weight):
        n_tok, width = tokens.shape
        units = gate_weight.shape[2]
        rows = nx * ROWS
        n_dc = width // DC
        half = nz // 2
        any_space = pl.BlockSpec(memory_space=pl.ANY)
        dma = pltpu.SemaphoreType.DMA
        return pl.pallas_call(
            functools.partial(body, nz, nx, ny),
            out_shape=jax.ShapeDtypeStruct((n_tok // ny, width), BF16),
            in_specs=[any_space] * 7,
            out_specs=pl.BlockSpec(memory_space=pltpu.VMEM),
            scratch_shapes=[
                pltpu.VMEM((3, nz, 128, units), BF16),
                pltpu.VMEM((n_tok, width), BF16),
                pltpu.VMEM((n_tok, width), BF16),
                pltpu.VMEM(routes.shape[::-1], jnp.int32),
                pltpu.VMEM(route_gates.shape[::-1], F32),
                pltpu.VMEM((nx, 48, width), BF16),
                pltpu.VMEM((nx - 1, 48, width), BF16),
                pltpu.VMEM((2, rows, width), BF16),
                pltpu.VMEM((3, rows, units), F32),
                pltpu.VMEM((2, rows, units), BF16),
                pltpu.VMEM((n_dc, nx - 1, 48, HC), BF16),
                pltpu.VMEM((n_dc, nx, 48, HC), BF16),
                pltpu.VMEM((n_dc, n_tok, DC), BF16),
                pltpu.VMEM((n_dc, 2, n_tok // ny, DC), BF16),
                pltpu.VMEM((n_dc, 2, n_tok // ny, HC), BF16),
                pltpu.VMEM((n_dc, 2, n_tok // ny, DC), BF16),
                pltpu.VMEM((n_dc, 4, n_tok // ny, DC), BF16),
                dma((4,)),
                dma((3,)),
                dma((half + 1, 3, 2)),
                dma((half + 1, 3, 2)),
                dma((half + 1, 3)),
                dma((half + 1, 3)),
                dma((2, nx)),
                dma((n_dc, nx)),
                dma((n_dc, nx)),
                dma((n_dc, 8)),
                dma((n_dc, 8)),
            ],
            compiler_params=pltpu.CompilerParams(
                collective_id=0, has_side_effects=True, vmem_limit_bytes=60 * 1024 * 1024
            ),
            cost_estimate=pl.CostEstimate(
                flops=10 * rows * width * units,
                bytes_accessed=16 * 1024 * 1024,
                transcendentals=rows * units,
            ),
            name="moe_input_grad",
        )(tokens, routes.T, route_gates.T, out_grad, gate_weight, up_weight, down_weight)

    return jax.shard_map(
        local,
        mesh=mesh,
        in_specs=(
            P(("dp", "node"), None),
            P(("dp", "node"), None),
            P(("dp", "node"), None),
            P(("dp", "node"), None),
            P(("node", "innode"), "dp", None),
            P(("node", "innode"), "dp", None),
            P(("node", "innode"), "dp", None),
        ),
        out_specs=P(("dp", "node", "innode"), None),
        check_vma=False,
    )
```

```python
import functools

import jax
import jax.numpy as jnp
from jax import lax
from jax.experimental import pallas as pl
from jax.experimental.pallas import tpu as pltpu
from jax.sharding import PartitionSpec as P

MESH = pl.DeviceIdType.MESH
F32 = jnp.float32
BF16 = jnp.bfloat16

ROWS = 24
SLOT = 32
NEAR = (0, -1, 1, 2, -2)
QUADS = 4


def body(
    nz, nx, ny,
    tok_hbm, routes_hbm, gates_hbm, grad_hbm, gate_hbm, up_hbm, down_hbm,
    out_ref,
    wbuf, tok, grd, rts, gts, xs, xr, lhs, acc, hid, spread, near_out, near_in, far_out, far_in, part, fin,
    in_sem, own_sem, z_send, z_recv, p_send, p_recv, x_sem, n_send, n_recv, f_send, f_recv, y_send, y_recv,
):
    half = nz // 2
    pairs = nz // 2
    dp = lax.axis_index("dp")
    x = lax.axis_index("node")
    y = lax.axis_index("innode")
    z, c = lax.div(dp, 2), lax.rem(dp, 2)
    nxt = lax.rem(z + 1, nz) * 2 + c
    prv = lax.rem(z + nz - 1, nz) * 2 + c
    ring = ({"dp": nxt}, {"dp": prv})
    partner = {"dp": z * 2 + 1 - c}
    x_to = [{"node": lax.rem(x + r, nx)} for r in range(nx)]
    y_at = [lax.rem(y + i, ny) for i in range(ny)]

    def back_to(r, step):
        return {"node": lax.rem(x + nx - r, nx), "innode": y_at[step % ny]}


    def mine(m, pos, count):
        return wbuf.at[m, pl.ds(pos, count), pl.ds(pl.multiple_of(c * 64, 64), 64), :]

    def piece(m, pos, s, d):
        if s == half:
            return wbuf.at[m, pos, pl.ds(pl.multiple_of(c * 64 + d * 32, 32), 32), :]
        return wbuf.at[m, pos, pl.ds(pl.multiple_of(c * 64, 64), 64), :]

    own = []
    for m, ref in enumerate((gate_hbm, up_hbm, down_hbm)):
        copy = pltpu.make_async_copy(ref, mine(m, 0, 1), own_sem.at[m])
        copy.start()
        own.append(copy)
    ins = []
    for i, (a, b) in enumerate(
        ((routes_hbm, rts), (gates_hbm, gts), (tok_hbm, tok), (grad_hbm, grd))
    ):
        copy = pltpu.make_async_copy(a, b, in_sem.at[i])
        copy.start()
        ins.append(copy)

    barrier = pltpu.get_barrier_semaphore()
    peers = [ring[0], ring[1], partner]
    peers += [back_to(r, i) for r in range(nx) for i in (-2, -1, 0, 1, 2) if r or i]
    peers += [back_to(0, i) for i in range(3, ny - 2)]
    for peer in peers:
        pl.semaphore_signal(barrier, inc=1, device_id=peer, device_id_type=MESH)
    pl.semaphore_wait(barrier, len(peers))

    def z_copy(s, m, d):
        return pltpu.make_async_remote_copy(
            src_ref=piece(m, place(s - 1, d), s, d),
            dst_ref=piece(m, place(s, d), s, d),
            send_sem=z_send.at[s, m, d],
            recv_sem=z_recv.at[s, m, d],
            device_id=ring[d],
            device_id_type=MESH,
        )

    def p_copy(s, m):
        ref = mine(m, 2 * s, 2) if 0 < s < half else mine(m, 0 if s == 0 else 1, 1)
        return pltpu.make_async_remote_copy(
            src_ref=ref,
            dst_ref=ref,
            send_sem=p_send.at[s, m],
            recv_sem=p_recv.at[s, m],
            device_id=partner,
            device_id_type=MESH,
        )

    sent = []

    def start(copy):
        copy.start()
        sent.append(copy)

    def place(s, d):
        return 0 if s == 0 else (1 if s == half else 2 * s + d)

    def service(s):
        for m in range(3):
            for d in range(2):
                z_copy(s, m, d).wait_recv()
                if s < half:
                    start(z_copy(s + 1, m, d))
            start(p_copy(s, m))

    for m in range(3):
        own[m].wait()
        for d in range(2):
            start(z_copy(1, m, d))
    for m in range(3):
        start(p_copy(0, m))

    ins[0].wait()
    ins[1].wait()
    n_tok = rts.shape[1]
    lanes = nx * SLOT
    line = lax.broadcasted_iota(jnp.int32, (lanes, n_tok), 0)
    slot = line & (SLOT - 1)
    slot1 = jnp.where(slot < 16, slot, jnp.where(slot >= 24, slot - 8, -1))
    group = x + (line >> 5)
    group = jnp.where(group >= nx, group - nx, group)
    earlier = (
        lax.broadcasted_iota(jnp.int32, (n_tok, n_tok), 0)
        < lax.broadcasted_iota(jnp.int32, (n_tok, n_tok), 1)
    ).astype(F32).astype(BF16)

    def find(step):
        expert = group * ny + y_at[step % ny]
        hit = jnp.zeros((lanes, n_tok), F32)
        weight = jnp.zeros((lanes, n_tok), F32)
        for k in range(rts.shape[0]):
            same = rts[k : k + 1, :] == expert
            hit = jnp.where(same, 1.0, hit)
            weight = jnp.where(same, gts[k : k + 1, :], weight)
        rank = jnp.dot(hit.astype(BF16), earlier, preferred_element_type=F32)
        own0 = jnp.where(rank == slot.astype(F32), hit, 0.0)
        own1 = jnp.where(rank == slot1.astype(F32), hit, 0.0)
        return own0, own1, weight

    def keep(i, rows):
        for h in range(2):
            spread[i, h] = jnp.transpose(rows[h]).astype(BF16)

    own_rows = find(0)
    pick = own_rows[0].astype(BF16)
    scale = jnp.sum(own_rows[0] * own_rows[2], axis=1, keepdims=True)

    ins[2].wait()
    ins[3].wait()
    for p in range(pairs):
        first = pl.multiple_of(lax.rem(z + nz - p, nz) * 128, 128)
        second = pl.multiple_of(lax.rem(z + (half if p == 0 else p), nz) * 128, 128)
        cols = pl.ds(p * 256, 256)
        a = jnp.concatenate([tok[:, pl.ds(first, 128)], tok[:, pl.ds(second, 128)]], axis=1)
        b = jnp.concatenate([grd[:, pl.ds(first, 128)], grd[:, pl.ds(second, 128)]], axis=1)
        a = jnp.dot(pick, a, preferred_element_type=F32)
        b = jnp.dot(pick, b, preferred_element_type=F32) * scale
        for r in range(nx):
            o = r * SLOT
            xs[r, 0:16, cols] = a[o : o + 16].astype(BF16)
            xs[r, 16:32, cols] = b[o : o + 16].astype(BF16)
            xs[r, 32:48, cols] = jnp.concatenate(
                [a[o + 16 : o + 24], b[o + 16 : o + 24]], axis=0
            ).astype(BF16)
    x_copies = []
    for r in range(1, nx):
        copy = pltpu.make_async_remote_copy(
            src_ref=xs.at[r],
            dst_ref=xr.at[r - 1],
            send_sem=x_sem.at[0, r],
            recv_sem=x_sem.at[1, r],
            device_id=x_to[r],
            device_id_type=MESH,
        )
        start(copy)
        x_copies.append(copy)

    keep(0, own_rows)

    def assemble():
        for copy in x_copies:
            copy.wait_recv()
        got = [xs.at[0]] + [xr.at[r - 1] for r in range(1, nx)]
        for r in range(nx):
            lhs[0, r * 16 : r * 16 + 16, :] = got[r][0:16, :]
            lhs[1, r * 16 : r * 16 + 16, :] = got[r][16:32, :]
        for r in range(0, nx, 2):
            a = got[r][32:48, :].astype(F32)
            b = got[r + 1][32:48, :].astype(F32)
            o = nx * 16 + r * 8
            lhs[0, o : o + 16, :] = jnp.concatenate([a[0:8], b[0:8]], axis=0).astype(BF16)
            lhs[1, o : o + 16, :] = jnp.concatenate([a[8:16], b[8:16]], axis=0).astype(BF16)

    def forward(p, m):
        if p == 0:
            p_copy(0, m).wait_recv()
            p_copy(half, m).wait_recv()
        else:
            p_copy(p, m).wait_recv()
        width = wbuf.shape[3]
        term = jnp.dot(
            lhs[m // 2, :, p * 256 : p * 256 + 256],
            wbuf[m, 2 * p : 2 * p + 2].reshape(256, width),
            preferred_element_type=F32,
        )
        if p == (1 if pairs > 1 else 0):
            acc[m] = term
        else:
            acc[m] += term

    wait_steps = min(3, half - 1)
    ready = []
    for s in range(1, half):
        service(s)
        if s == wait_steps:
            assemble()
        if s >= wait_steps:
            while ready:
                p = ready.pop(0)
                for m in range(3):
                    forward(p, m)
            if s > wait_steps:
                i = s - wait_steps
                keep(i, find(NEAR[i]))
        ready.append(s)
    for p in ready:
        for m in range(3):
            forward(p, m)
    service(half)
    forward(0, 0)
    forward(0, 1)
    gate_pre, up_pre = acc[0], acc[1]
    sigma = 1.0 / (1.0 + jnp.exp(-gate_pre))
    acc[0] = up_pre * sigma * (1.0 + gate_pre * (1.0 - sigma))
    acc[1] = gate_pre * sigma
    forward(0, 2)
    hidden = acc[2]
    hid[0] = (hidden * acc[0]).astype(BF16)
    hid[1] = (hidden * acc[1]).astype(BF16)

    over = (((1,), (1,)), ((), ()))

    def backward(p):
        term = None
        for m in range(2):
            rhs = wbuf[m, pl.ds(2 * p, 2)].reshape(256, wbuf.shape[3])
            part_sum = lax.dot_general(hid[m], rhs, over, preferred_element_type=F32)
            term = part_sum if term is None else term + part_sum
        return term

    def fold(dest, a, b):
        def put(r):
            o, q = r * 16, nx * 16 + r * 8
            dest(r)[0:16, :] = a[o : o + 16].astype(BF16)
            dest(r)[16:32, :] = b[o : o + 16].astype(BF16)
            dest(r)[32:48, :] = jnp.concatenate([a[q : q + 8], b[q : q + 8]], axis=0).astype(BF16)

        return put

    def near_copy(i, r):
        return pltpu.make_async_remote_copy(
            src_ref=near_out.at[i, r],
            dst_ref=near_in.at[i, r],
            send_sem=n_send.at[i, r],
            recv_sem=n_recv.at[i, r],
            device_id=back_to(r, -NEAR[i]),
            device_id_type=MESH,
        )

    def far_copy(h, r):
        return pltpu.make_async_remote_copy(
            src_ref=far_out.at[h, r],
            dst_ref=far_in.at[h, r],
            send_sem=f_send.at[h, r],
            recv_sem=f_recv.at[h, r],
            device_id=back_to(r, -NEAR[3 + h]),
            device_id_type=MESH,
        )

    across = (2, 1, 3, 0)
    quad = [lax.rem(y + k, QUADS) for k in range(QUADS)]
    for h in range(2):
        a = backward(2 * quad[2] + h)
        put = fold(lambda r: far_out.at[h, r], a[:, :128], a[:, 128:])
        for r in across:
            put(r)
            start(far_copy(h, r))
    for i, k in ((1, 1), (2, 3), (0, 0)):
        a, b = backward(2 * quad[k]), backward(2 * quad[k] + 1)
        put = fold(lambda r: near_out.at[i, r] if r or i else near_in.at[0, 0], a, b)
        for r in across:
            put(r)
            if r or i:
                start(near_copy(i, r))

    for i in (0, 1, 2):
        for r in range(nx):
            if r or i:
                near_copy(i, r).wait_recv()
    for h in range(2):
        for r in range(nx):
            far_copy(h, r).wait_recv()
        total = None
        for i in (0, 1, 2):
            rows = []
            for r in range(nx):
                rows += [near_in[i, r, h * 16 : h * 16 + 16, :], near_in[i, r, 32:48, :]]
            term = jnp.dot(
                spread[i, h], jnp.concatenate(rows, axis=0), preferred_element_type=F32
            )
            total = term if total is None else total + term
        rows = []
        for r in range(nx):
            rest = far_in[h, r, 32:48, :].astype(F32)
            rest = jnp.concatenate([rest[0:8], rest[8:16]], axis=1)
            rows += [
                jnp.concatenate([far_in[h, r, 0:16, :], far_in[h, r, 16:32, :]], axis=1),
                jnp.concatenate([rest, jnp.zeros_like(rest)], axis=0).astype(BF16),
            ]
        total += jnp.dot(
            spread[3 + h, 0], jnp.concatenate(rows, axis=0), preferred_element_type=F32
        )
        part[h] = total.astype(BF16)

    def rows_of(i):
        return pl.ds(pl.multiple_of(y_at[i] * 16, 16), 16)

    def y_copy(i):
        return pltpu.make_async_remote_copy(
            src_ref=part.at[:, rows_of(i), :],
            dst_ref=fin.at[i - 1],
            send_sem=y_send.at[i],
            recv_sem=y_recv.at[i],
            device_id=back_to(0, i),
            device_id_type=MESH,
        )

    for i in (4, 3, 5, 2, 6, 1, 7):
        start(y_copy(i))
    for i in (1, 2, 3, 0):
        if i:
            y_copy(i).wait_recv()
        y_copy(i + 4).wait_recv()
        q = lax.rem(y + ny - i, QUADS)
        for h in range(2):
            mine_too = fin[i - 1, h] if i else part[h, rows_of(0), :]
            total = (mine_too.astype(F32) + fin[i + 3, h].astype(F32)).astype(BF16)
            p = 2 * q + h
            for side, src in enumerate((z + nz - p, z + jnp.where(p == 0, half, p))):
                cols = pl.ds(pl.multiple_of(lax.rem(src, nz) * 128, 128), 128)
                out_ref[:, cols] = total[:, side * 128 : side * 128 + 128]
    for copy in sent:
        copy.wait_send()


def solution(mesh):
    nz, nx, ny = mesh.shape["dp"] // 2, mesh.shape["node"], mesh.shape["innode"]

    def local(tokens, routes, route_gates, out_grad, gate_weight, up_weight, down_weight):
        n_tok, width = tokens.shape
        units = gate_weight.shape[2]
        rows = nx * ROWS
        assert (nx, ny, nz, width, n_tok) == (4, 8, 16, 2048, 128)
        half = nz // 2
        any_space = pl.BlockSpec(memory_space=pl.ANY)
        dma = pltpu.SemaphoreType.DMA
        return pl.pallas_call(
            functools.partial(body, nz, nx, ny),
            out_shape=jax.ShapeDtypeStruct((n_tok // ny, width), BF16),
            in_specs=[any_space] * 7,
            out_specs=pl.BlockSpec(memory_space=pltpu.VMEM),
            scratch_shapes=[
                pltpu.VMEM((3, nz, 128, units), BF16),
                pltpu.VMEM((n_tok, width), BF16),
                pltpu.VMEM((n_tok, width), BF16),
                pltpu.VMEM(routes.shape[::-1], jnp.int32),
                pltpu.VMEM(route_gates.shape[::-1], F32),
                pltpu.VMEM((nx, 48, width), BF16),
                pltpu.VMEM((nx - 1, 48, width), BF16),
                pltpu.VMEM((2, rows, width), BF16),
                pltpu.VMEM((3, rows, units), F32),
                pltpu.VMEM((2, rows, units), BF16),
                pltpu.VMEM((5, 2, n_tok, nx * SLOT), BF16),
                pltpu.VMEM((3, nx, 48, 256), BF16),
                pltpu.VMEM((3, nx, 48, 256), BF16),
                pltpu.VMEM((2, nx, 48, 128), BF16),
                pltpu.VMEM((2, nx, 48, 128), BF16),
                pltpu.VMEM((2, n_tok, 256), BF16),
                pltpu.VMEM((ny - 1, 2, n_tok // ny, 256), BF16),
                dma((4,)),
                dma((3,)),
                dma((half + 1, 3, 2)),
                dma((half + 1, 3, 2)),
                dma((half + 1, 3)),
                dma((half + 1, 3)),
                dma((2, nx)),
                dma((3, nx)),
                dma((3, nx)),
                dma((2, nx)),
                dma((2, nx)),
                dma((ny,)),
                dma((ny,)),
            ],
            compiler_params=pltpu.CompilerParams(
                collective_id=0, has_side_effects=True, vmem_limit_bytes=60 * 1024 * 1024
            ),
            cost_estimate=pl.CostEstimate(
                flops=10 * rows * width * units,
                bytes_accessed=16 * 1024 * 1024,
                transcendentals=rows * units,
            ),
            name="moe_input_grad",
        )(tokens, routes.T, route_gates.T, out_grad, gate_weight, up_weight, down_weight)

    return jax.shard_map(
        local,
        mesh=mesh,
        in_specs=(
            P(("dp", "node"), None),
            P(("dp", "node"), None),
            P(("dp", "node"), None),
            P(("dp", "node"), None),
            P(("node", "innode"), "dp", None),
            P(("node", "innode"), "dp", None),
            P(("node", "innode"), "dp", None),
        ),
        out_specs=P(("dp", "node", "innode"), None),
        check_vma=False,
    )
```

```python
import functools

import jax
import jax.numpy as jnp
from jax import lax
from jax.experimental import pallas as pl
from jax.experimental.pallas import tpu as pltpu
from jax.sharding import PartitionSpec as P

MESH = pl.DeviceIdType.MESH
F32 = jnp.float32
BF16 = jnp.bfloat16

ROWS = 24
SLOT = 32
NEAR = (0, -1, 1, 2, -2)
QUADS = 4


def body(
    nz, nx, ny,
    tok_hbm, routes_hbm, gates_hbm, grad_hbm, gate_hbm, up_hbm, down_hbm,
    out_ref,
    wbuf, tok, grd, rts, gts, xs, xr, lhs, acc, hid, spread, near_out, near_in, far_out, far_in, part,
    in_sem, own_sem, z_send, z_recv, e_send, e_recv, p_send, p_recv, x_sem, n_send, n_recv, f_send, f_recv, y_send, y_recv,
):
    half = nz // 2
    pairs = nz // 2
    dp = lax.axis_index("dp")
    x = lax.axis_index("node")
    y = lax.axis_index("innode")
    z, c = lax.div(dp, 2), lax.rem(dp, 2)
    nxt = lax.rem(z + 1, nz) * 2 + c
    prv = lax.rem(z + nz - 1, nz) * 2 + c
    ring = ({"dp": nxt}, {"dp": prv})
    partner = {"dp": z * 2 + 1 - c}
    cross = ({"dp": nxt + 1 - 2 * c}, {"dp": prv + 1 - 2 * c})
    x_to = [{"node": lax.rem(x + r, nx)} for r in range(nx)]
    y_at = [lax.rem(y + i, ny) for i in range(ny)]

    def back_to(r, step):
        return {"node": lax.rem(x + nx - r, nx), "innode": y_at[step % ny]}


    def mine(m, pos, count):
        return wbuf.at[m, pl.ds(pos, count), pl.ds(pl.multiple_of(c * 64, 64), 64), :]

    def piece(m, pos, s, d):
        if s == half:
            return wbuf.at[m, pos, pl.ds(pl.multiple_of(c * 64 + d * 32, 32), 32), :]
        return wbuf.at[m, pos, pl.ds(pl.multiple_of(c * 64, 64), 64), :]

    own = []
    for m, ref in enumerate((gate_hbm, up_hbm, down_hbm)):
        copy = pltpu.make_async_copy(ref, mine(m, 0, 1), own_sem.at[m])
        copy.start()
        own.append(copy)
    ins = []
    for i, (a, b) in enumerate(
        ((routes_hbm, rts), (gates_hbm, gts), (tok_hbm, tok), (grad_hbm, grd))
    ):
        copy = pltpu.make_async_copy(a, b, in_sem.at[i])
        copy.start()
        ins.append(copy)

    barrier = pltpu.get_barrier_semaphore()
    peers = [ring[0], ring[1], partner, cross[0], cross[1]]
    peers += [back_to(r, i) for r in range(nx) for i in (-2, -1, 0, 1, 2) if r or i]
    peers += [back_to(0, i) for i in range(3, ny - 2)]
    for peer in peers:
        pl.semaphore_signal(barrier, inc=1, device_id=peer, device_id_type=MESH)
    pl.semaphore_wait(barrier, len(peers))

    def z_copy(s, m, d):
        return pltpu.make_async_remote_copy(
            src_ref=piece(m, place(s - 1, d), s, d),
            dst_ref=piece(m, place(s, d), s, d),
            send_sem=z_send.at[s, m, d],
            recv_sem=z_recv.at[s, m, d],
            device_id=ring[d],
            device_id_type=MESH,
        )

    def e_copy(d):
        return pltpu.make_async_remote_copy(
            src_ref=piece(2, place(half - 1, d), half, d),
            dst_ref=piece(2, place(half, d), half, d),
            send_sem=e_send.at[d],
            recv_sem=e_recv.at[d],
            device_id=cross[d],
            device_id_type=MESH,
        )

    def p_copy(s, m):
        ref = mine(m, 2 * s, 2) if 0 < s < half else mine(m, 0 if s == 0 else 1, 1)
        return pltpu.make_async_remote_copy(
            src_ref=ref,
            dst_ref=ref,
            send_sem=p_send.at[s, m],
            recv_sem=p_recv.at[s, m],
            device_id=partner,
            device_id_type=MESH,
        )

    sent = []

    def start(copy):
        copy.start()
        sent.append(copy)

    def place(s, d):
        return 0 if s == 0 else (1 if s == half else 2 * s + d)

    def service(s):
        for m in range(3):
            for d in range(2):
                z_copy(s, m, d).wait_recv()
                if s < half:
                    start(z_copy(s + 1, m, d))
                if s + 1 == half and m == 2:
                    start(e_copy(d))
            if s < half or m < 2:
                start(p_copy(s, m))

    for m in range(3):
        own[m].wait()
        for d in range(2):
            start(z_copy(1, m, d))
    for m in range(3):
        start(p_copy(0, m))

    ins[0].wait()
    ins[1].wait()
    n_tok = rts.shape[1]
    lanes = nx * SLOT
    line = lax.broadcasted_iota(jnp.int32, (lanes, n_tok), 0)
    slot = line & (SLOT - 1)
    slot1 = jnp.where(slot < 16, slot, jnp.where(slot >= 24, slot - 8, -1))
    group = x + (line >> 5)
    group = jnp.where(group >= nx, group - nx, group)
    earlier = (
        lax.broadcasted_iota(jnp.int32, (n_tok, n_tok), 0)
        < lax.broadcasted_iota(jnp.int32, (n_tok, n_tok), 1)
    ).astype(F32).astype(BF16)

    def find(step):
        expert = group * ny + y_at[step % ny]
        hit = jnp.zeros((lanes, n_tok), F32)
        weight = jnp.zeros((lanes, n_tok), F32)
        for k in range(rts.shape[0]):
            same = rts[k : k + 1, :] == expert
            hit = jnp.where(same, 1.0, hit)
            weight = jnp.where(same, gts[k : k + 1, :], weight)
        rank = jnp.dot(hit.astype(BF16), earlier, preferred_element_type=F32)
        own0 = jnp.where(rank == slot.astype(F32), hit, 0.0)
        own1 = jnp.where(rank == slot1.astype(F32), hit, 0.0)
        return own0, own1, weight

    def keep(i, rows):
        for h in range(2):
            spread[i, h] = jnp.transpose(rows[h]).astype(BF16)

    own_rows = find(0)
    pick = own_rows[0].astype(BF16)
    scale = jnp.sum(own_rows[0] * own_rows[2], axis=1, keepdims=True)

    ins[2].wait()
    ins[3].wait()
    for p in range(pairs):
        first = pl.multiple_of(lax.rem(z + nz - p, nz) * 128, 128)
        second = pl.multiple_of(lax.rem(z + (half if p == 0 else p), nz) * 128, 128)
        cols = pl.ds(p * 256, 256)
        a = jnp.concatenate([tok[:, pl.ds(first, 128)], tok[:, pl.ds(second, 128)]], axis=1)
        b = jnp.concatenate([grd[:, pl.ds(first, 128)], grd[:, pl.ds(second, 128)]], axis=1)
        a = jnp.dot(pick, a, preferred_element_type=F32)
        b = jnp.dot(pick, b, preferred_element_type=F32) * scale
        for r in range(nx):
            o = r * SLOT
            xs[r, 0:16, cols] = a[o : o + 16].astype(BF16)
            xs[r, 16:32, cols] = b[o : o + 16].astype(BF16)
            xs[r, 32:48, cols] = jnp.concatenate(
                [a[o + 16 : o + 24], b[o + 16 : o + 24]], axis=0
            ).astype(BF16)
    x_copies = []
    for r in range(1, nx):
        copy = pltpu.make_async_remote_copy(
            src_ref=xs.at[r],
            dst_ref=xr.at[r - 1],
            send_sem=x_sem.at[0, r],
            recv_sem=x_sem.at[1, r],
            device_id=x_to[r],
            device_id_type=MESH,
        )
        start(copy)
        x_copies.append(copy)

    keep(0, own_rows)

    def assemble():
        for copy in x_copies:
            copy.wait_recv()
        got = [xs.at[0]] + [xr.at[r - 1] for r in range(1, nx)]
        for r in range(nx):
            lhs[0, r * 16 : r * 16 + 16, :] = got[r][0:16, :]
            lhs[1, r * 16 : r * 16 + 16, :] = got[r][16:32, :]
        for r in range(0, nx, 2):
            a = got[r][32:48, :].astype(F32)
            b = got[r + 1][32:48, :].astype(F32)
            o = nx * 16 + r * 8
            lhs[0, o : o + 16, :] = jnp.concatenate([a[0:8], b[0:8]], axis=0).astype(BF16)
            lhs[1, o : o + 16, :] = jnp.concatenate([a[8:16], b[8:16]], axis=0).astype(BF16)

    def add(m, pos, count, fresh=False):
        term = jnp.dot(
            lhs[m // 2, :, pos * 128 : (pos + count) * 128],
            wbuf[m, pos : pos + count].reshape(count * 128, wbuf.shape[3]),
            preferred_element_type=F32,
        )
        if fresh:
            acc[m] = term
        else:
            acc[m] += term

    def forward(p, m):
        p_copy(p, m).wait_recv()
        add(m, 2 * p, 2, p == 1)

    def forward_last(m):
        if m < 2:
            p_copy(half, m).wait_recv()
            p_copy(0, m).wait_recv()
            add(m, 0, 2)
        else:
            e_copy(0).wait_recv()
            e_copy(1).wait_recv()
            add(m, 1, 1)

    wait_steps = min(3, half - 1)
    ready = []
    for s in range(1, half):
        service(s)
        if s == wait_steps:
            assemble()
        if s >= wait_steps:
            while ready:
                p = ready.pop(0)
                for m in range(3):
                    forward(p, m)
            if s > wait_steps:
                i = s - wait_steps
                keep(i, find(NEAR[i]))
        ready.append(s)
    for p in ready:
        for m in range(3):
            forward(p, m)
    p_copy(0, 2).wait_recv()
    add(2, 0, 1)
    service(half)
    forward_last(0)
    forward_last(1)
    gate_pre, up_pre = acc[0], acc[1]
    sigma = 1.0 / (1.0 + jnp.exp(-gate_pre))
    acc[0] = up_pre * sigma * (1.0 + gate_pre * (1.0 - sigma))
    acc[1] = gate_pre * sigma
    forward_last(2)
    hidden = acc[2]
    hid[0] = (hidden * acc[0]).astype(BF16)
    hid[1] = (hidden * acc[1]).astype(BF16)

    over = (((1,), (1,)), ((), ()))

    def held(block):
        away = lax.rem(z + nz - block, nz)
        low = jnp.where(away == 0, 0, 2 * away)
        return jnp.where(away < half, low, jnp.where(away == half, 1, 2 * (nz - away) + 1))

    def backward(p):
        term = None
        first, second = held(2 * p), held(2 * p + 1)
        for m in range(2):
            rhs = jnp.concatenate([wbuf[m, first], wbuf[m, second]], axis=0)
            part_sum = lax.dot_general(hid[m], rhs, over, preferred_element_type=F32)
            term = part_sum if term is None else term + part_sum
        return term

    def fold(dest, a, b):
        def put(r):
            o, q = r * 16, nx * 16 + r * 8
            dest(r)[0:16, :] = a[o : o + 16].astype(BF16)
            dest(r)[16:32, :] = b[o : o + 16].astype(BF16)
            dest(r)[32:48, :] = jnp.concatenate([a[q : q + 8], b[q : q + 8]], axis=0).astype(BF16)

        return put

    def near_copy(i, r):
        return pltpu.make_async_remote_copy(
            src_ref=near_out.at[i, r],
            dst_ref=near_in.at[i, r],
            send_sem=n_send.at[i, r],
            recv_sem=n_recv.at[i, r],
            device_id=back_to(r, -NEAR[i]),
            device_id_type=MESH,
        )

    def far_copy(h, r):
        return pltpu.make_async_remote_copy(
            src_ref=far_out.at[h, r],
            dst_ref=far_in.at[h, r],
            send_sem=f_send.at[h, r],
            recv_sem=f_recv.at[h, r],
            device_id=back_to(r, -NEAR[3 + h]),
            device_id_type=MESH,
        )

    across = (2, 1, 3, 0)
    quad = [lax.rem(y + k, QUADS) for k in range(QUADS)]
    for h in range(2):
        a = backward(2 * quad[2] + h)
        put = fold(lambda r: far_out.at[h, r], a[:, :128], a[:, 128:])
        for r in across:
            put(r)
            start(far_copy(h, r))
    for i, k in ((1, 1), (2, 3), (0, 0)):
        a, b = backward(2 * quad[k]), backward(2 * quad[k] + 1)
        put = fold(lambda r: near_out.at[i, r] if r or i else near_in.at[0, 0], a, b)
        for r in across:
            put(r)
            if r or i:
                start(near_copy(i, r))

    sums = []
    for h in range(2):
        rows = []
        for r in range(nx):
            far_copy(h, r).wait_recv()
            rest = far_in[h, r, 32:48, :].astype(F32)
            rest = jnp.concatenate([rest[0:8], rest[8:16]], axis=1)
            rows += [
                jnp.concatenate([far_in[h, r, 0:16, :], far_in[h, r, 16:32, :]], axis=1),
                jnp.concatenate([rest, jnp.zeros_like(rest)], axis=0).astype(BF16),
            ]
        sums.append(
            jnp.dot(
                spread[3 + h, 0], jnp.concatenate(rows, axis=0), preferred_element_type=F32
            )
        )
    for i in (1, 2, 0):
        for r in range(nx):
            if r or i:
                near_copy(i, r).wait_recv()
        for h in range(2):
            rows = []
            for r in range(nx):
                rows += [near_in[i, r, h * 16 : h * 16 + 16, :], near_in[i, r, 32:48, :]]
            sums[h] += jnp.dot(
                spread[i, h], jnp.concatenate(rows, axis=0), preferred_element_type=F32
            )
    for h in range(2):
        part[:, h * 256 : h * 256 + 256] = sums[h].astype(BF16)

    def rows_of(i):
        return pl.ds(pl.multiple_of(y_at[i] * 16, 16), 16)

    place_out = out_ref.at[
        lax.div(y, QUADS), :, pl.ds(pl.multiple_of(quad[0] * 512, 512), 512)
    ]

    def y_copy(i):
        return pltpu.make_async_remote_copy(
            src_ref=part.at[rows_of(i), :],
            dst_ref=place_out,
            send_sem=y_send.at[i],
            recv_sem=y_recv.at[i],
            device_id=back_to(0, i),
            device_id_type=MESH,
        )

    for i in (4, 3, 5, 2, 6, 1, 7):
        start(y_copy(i))
    kept = pltpu.make_async_copy(part.at[rows_of(0), :], place_out, y_send.at[0])
    kept.start()
    for i in range(1, ny):
        y_copy(i).wait_recv()
    kept.wait()
    for copy in sent:
        copy.wait_send()


def solution(mesh):
    nz, nx, ny = mesh.shape["dp"] // 2, mesh.shape["node"], mesh.shape["innode"]

    def local(tokens, routes, route_gates, out_grad, gate_weight, up_weight, down_weight):
        n_tok, width = tokens.shape
        units = gate_weight.shape[2]
        rows = nx * ROWS
        assert (nx, ny, nz, width, n_tok) == (4, 8, 16, 2048, 128)
        half = nz // 2
        any_space = pl.BlockSpec(memory_space=pl.ANY)
        dma = pltpu.SemaphoreType.DMA
        halves = pl.pallas_call(
            functools.partial(body, nz, nx, ny),
            out_shape=jax.ShapeDtypeStruct((2, n_tok // ny, width), BF16),
            in_specs=[any_space] * 7,
            out_specs=any_space,
            scratch_shapes=[
                pltpu.VMEM((3, nz, 128, units), BF16),
                pltpu.VMEM((n_tok, width), BF16),
                pltpu.VMEM((n_tok, width), BF16),
                pltpu.VMEM(routes.shape[::-1], jnp.int32),
                pltpu.VMEM(route_gates.shape[::-1], F32),
                pltpu.VMEM((nx, 48, width), BF16),
                pltpu.VMEM((nx - 1, 48, width), BF16),
                pltpu.VMEM((2, rows, width), BF16),
                pltpu.VMEM((3, rows, units), F32),
                pltpu.VMEM((2, rows, units), BF16),
                pltpu.VMEM((5, 2, n_tok, nx * SLOT), BF16),
                pltpu.VMEM((3, nx, 48, 256), BF16),
                pltpu.VMEM((3, nx, 48, 256), BF16),
                pltpu.VMEM((2, nx, 48, 128), BF16),
                pltpu.VMEM((2, nx, 48, 128), BF16),
                pltpu.VMEM((n_tok, 512), BF16),
                dma((4,)),
                dma((3,)),
                dma((half + 1, 3, 2)),
                dma((half + 1, 3, 2)),
                dma((2,)),
                dma((2,)),
                dma((half + 1, 3)),
                dma((half + 1, 3)),
                dma((2, nx)),
                dma((3, nx)),
                dma((3, nx)),
                dma((2, nx)),
                dma((2, nx)),
                dma((ny,)),
                dma((ny,)),
            ],
            compiler_params=pltpu.CompilerParams(
                collective_id=0, has_side_effects=True, vmem_limit_bytes=60 * 1024 * 1024
            ),
            cost_estimate=pl.CostEstimate(
                flops=10 * rows * width * units,
                bytes_accessed=16 * 1024 * 1024,
                transcendentals=rows * units,
            ),
            name="moe_input_grad",
        )(tokens, routes.T, route_gates.T, out_grad, gate_weight, up_weight, down_weight)
        return (halves[0].astype(F32) + halves[1].astype(F32)).astype(BF16)

    return jax.shard_map(
        local,
        mesh=mesh,
        in_specs=(
            P(("dp", "node"), None),
            P(("dp", "node"), None),
            P(("dp", "node"), None),
            P(("dp", "node"), None),
            P(("node", "innode"), "dp", None),
            P(("node", "innode"), "dp", None),
            P(("node", "innode"), "dp", None),
        ),
        out_specs=P(("dp", "node", "innode"), None),
        check_vma=False,
    )
```

```python
import functools

import jax
import jax.numpy as jnp
from jax import lax
from jax.experimental import pallas as pl
from jax.experimental.pallas import tpu as pltpu
from jax.sharding import PartitionSpec as P

MESH = pl.DeviceIdType.MESH
F32 = jnp.float32
BF16 = jnp.bfloat16

ROWS = 24
SLOT = 32
NEAR = (0, -1, 1, 2, -2)
QUADS = 4


def body(
    nz, nx, ny,
    tok_hbm, routes_hbm, gates_hbm, grad_hbm, gate_hbm, up_hbm, down_hbm,
    out_ref,
    wbuf, tok, grd, rts, gts, xs, xr, lhs, acc, hid, spread, near_out, near_in, far_out, far_in, part,
    in_sem, own_sem, z_send, z_recv, e_send, e_recv, p_send, p_recv, x_sem, n_send, n_recv, f_send, f_recv, y_send, y_recv,
):
    half = nz // 2
    pairs = nz // 2
    dp = lax.axis_index("dp")
    x = lax.axis_index("node")
    y = lax.axis_index("innode")
    z, c = lax.div(dp, 2), lax.rem(dp, 2)
    nxt = lax.rem(z + 1, nz) * 2 + c
    prv = lax.rem(z + nz - 1, nz) * 2 + c
    ring = ({"dp": nxt}, {"dp": prv})
    partner = {"dp": z * 2 + 1 - c}
    cross = ({"dp": nxt + 1 - 2 * c}, {"dp": prv + 1 - 2 * c})
    x_to = [{"node": lax.rem(x + r, nx)} for r in range(nx)]
    y_at = [lax.rem(y + i, ny) for i in range(ny)]

    def back_to(r, step):
        return {"node": lax.rem(x + nx - r, nx), "innode": y_at[step % ny]}


    def mine(m, pos, count):
        return wbuf.at[m, pl.ds(pos, count), pl.ds(pl.multiple_of(c * 64, 64), 64), :]

    def piece(m, pos, s, d):
        if s == half:
            return wbuf.at[m, pos, pl.ds(pl.multiple_of(c * 64 + d * 32, 32), 32), :]
        return wbuf.at[m, pos, pl.ds(pl.multiple_of(c * 64, 64), 64), :]

    own = []
    for m, ref in enumerate((gate_hbm, up_hbm, down_hbm)):
        copy = pltpu.make_async_copy(ref, mine(m, 0, 1), own_sem.at[m])
        copy.start()
        own.append(copy)
    ins = []
    for i, (a, b) in enumerate(
        ((routes_hbm, rts), (gates_hbm, gts), (tok_hbm, tok), (grad_hbm, grd))
    ):
        copy = pltpu.make_async_copy(a, b, in_sem.at[i])
        copy.start()
        ins.append(copy)

    barrier = pltpu.get_barrier_semaphore()
    peers = [ring[0], ring[1], partner, cross[0], cross[1]]
    peers += [back_to(r, i) for r in range(nx) for i in (-2, -1, 0, 1, 2) if r or i]
    peers += [back_to(0, i) for i in range(3, ny - 2)]
    for peer in peers:
        pl.semaphore_signal(barrier, inc=1, device_id=peer, device_id_type=MESH)
    pl.semaphore_wait(barrier, len(peers))

    def z_copy(s, m, d):
        return pltpu.make_async_remote_copy(
            src_ref=piece(m, place(s - 1, d), s, d),
            dst_ref=piece(m, place(s, d), s, d),
            send_sem=z_send.at[s, m, d],
            recv_sem=z_recv.at[s, m, d],
            device_id=ring[d],
            device_id_type=MESH,
        )

    def e_copy(d):
        return pltpu.make_async_remote_copy(
            src_ref=piece(2, place(half - 1, d), half, d),
            dst_ref=piece(2, place(half, d), half, d),
            send_sem=e_send.at[d],
            recv_sem=e_recv.at[d],
            device_id=cross[d],
            device_id_type=MESH,
        )

    def p_copy(s, m):
        ref = mine(m, 2 * s, 2) if 0 < s < half else mine(m, 0 if s == 0 else 1, 1)
        return pltpu.make_async_remote_copy(
            src_ref=ref,
            dst_ref=ref,
            send_sem=p_send.at[s, m],
            recv_sem=p_recv.at[s, m],
            device_id=partner,
            device_id_type=MESH,
        )

    sent = []

    def start(copy):
        copy.start()
        sent.append(copy)

    def place(s, d):
        return 0 if s == 0 else (1 if s == half else 2 * s + d)

    def service(s):
        for m in range(3):
            for d in range(2):
                z_copy(s, m, d).wait_recv()
                if s < half:
                    start(z_copy(s + 1, m, d))
                if s + 1 == half and m == 2:
                    start(e_copy(d))
            if s < half or m < 2:
                start(p_copy(s, m))

    for m in range(3):
        own[m].wait()
        for d in range(2):
            start(z_copy(1, m, d))
    for m in range(3):
        start(p_copy(0, m))

    ins[0].wait()
    ins[1].wait()
    n_tok = rts.shape[1]
    lanes = nx * SLOT
    line = lax.broadcasted_iota(jnp.int32, (lanes, n_tok), 0)
    slot = line & (SLOT - 1)
    slot1 = jnp.where(slot < 16, slot, jnp.where(slot >= 24, slot - 8, -1))
    group = x + (line >> 5)
    group = jnp.where(group >= nx, group - nx, group)
    earlier = (
        lax.broadcasted_iota(jnp.int32, (n_tok, n_tok), 0)
        < lax.broadcasted_iota(jnp.int32, (n_tok, n_tok), 1)
    ).astype(F32).astype(BF16)

    def find(step):
        expert = group * ny + y_at[step % ny]
        hit = jnp.zeros((lanes, n_tok), F32)
        weight = jnp.zeros((lanes, n_tok), F32)
        for k in range(rts.shape[0]):
            same = rts[k : k + 1, :] == expert
            hit = jnp.where(same, 1.0, hit)
            weight = jnp.where(same, gts[k : k + 1, :], weight)
        rank = jnp.dot(hit.astype(BF16), earlier, preferred_element_type=F32)
        own0 = jnp.where(rank == slot.astype(F32), hit, 0.0)
        own1 = jnp.where(rank == slot1.astype(F32), hit, 0.0)
        return own0, own1, weight

    def keep(i, rows):
        for h in range(2):
            spread[i, h] = jnp.transpose(rows[h]).astype(BF16)

    own_rows = find(0)
    pick = own_rows[0].astype(BF16)
    scale = jnp.sum(own_rows[0] * own_rows[2], axis=1, keepdims=True)

    ins[2].wait()
    ins[3].wait()
    for p in range(pairs):
        first = pl.multiple_of(lax.rem(z + nz - p, nz) * 128, 128)
        second = pl.multiple_of(lax.rem(z + (half if p == 0 else p), nz) * 128, 128)
        cols = pl.ds(p * 256, 256)
        a = jnp.concatenate([tok[:, pl.ds(first, 128)], tok[:, pl.ds(second, 128)]], axis=1)
        b = jnp.concatenate([grd[:, pl.ds(first, 128)], grd[:, pl.ds(second, 128)]], axis=1)
        a = jnp.dot(pick, a, preferred_element_type=F32)
        b = jnp.dot(pick, b, preferred_element_type=F32) * scale
        for r in range(nx):
            o = r * SLOT
            xs[r, 0:16, cols] = a[o : o + 16].astype(BF16)
            xs[r, 16:32, cols] = b[o : o + 16].astype(BF16)
            xs[r, 32:48, cols] = jnp.concatenate(
                [a[o + 16 : o + 24], b[o + 16 : o + 24]], axis=0
            ).astype(BF16)
    x_copies = []
    for r in range(1, nx):
        copy = pltpu.make_async_remote_copy(
            src_ref=xs.at[r],
            dst_ref=xr.at[r - 1],
            send_sem=x_sem.at[0, r],
            recv_sem=x_sem.at[1, r],
            device_id=x_to[r],
            device_id_type=MESH,
        )
        start(copy)
        x_copies.append(copy)

    keep(0, own_rows)

    def assemble():
        for copy in x_copies:
            copy.wait_recv()
        got = [xs.at[0]] + [xr.at[r - 1] for r in range(1, nx)]
        for r in range(nx):
            lhs[0, r * 16 : r * 16 + 16, :] = got[r][0:16, :]
            lhs[1, r * 16 : r * 16 + 16, :] = got[r][16:32, :]
        for r in range(0, nx, 2):
            a = got[r][32:48, :].astype(F32)
            b = got[r + 1][32:48, :].astype(F32)
            o = nx * 16 + r * 8
            lhs[0, o : o + 16, :] = jnp.concatenate([a[0:8], b[0:8]], axis=0).astype(BF16)
            lhs[1, o : o + 16, :] = jnp.concatenate([a[8:16], b[8:16]], axis=0).astype(BF16)

    def add(m, pos, count, fresh=False):
        term = jnp.dot(
            lhs[m // 2, :, pos * 128 : (pos + count) * 128],
            wbuf[m, pos : pos + count].reshape(count * 128, wbuf.shape[3]),
            preferred_element_type=F32,
        )
        if fresh:
            acc[m] = term
        else:
            acc[m] += term

    def forward(p, m):
        p_copy(p, m).wait_recv()
        add(m, 2 * p, 2, p == 1)

    def forward_last(m):
        if m < 2:
            p_copy(half, m).wait_recv()
            p_copy(0, m).wait_recv()
            add(m, 0, 2)
        else:
            e_copy(0).wait_recv()
            e_copy(1).wait_recv()
            add(m, 1, 1)

    wait_steps = min(3, half - 1)
    ready = []
    for s in range(1, half):
        service(s)
        if s == wait_steps:
            assemble()
        if s >= wait_steps:
            while ready:
                p = ready.pop(0)
                for m in range(3):
                    forward(p, m)
            if s > wait_steps:
                i = s - wait_steps
                keep(i, find(NEAR[i]))
        ready.append(s)
    for p in ready:
        for m in range(3):
            forward(p, m)
    p_copy(0, 2).wait_recv()
    add(2, 0, 1)
    service(half)
    forward_last(0)
    forward_last(1)
    gate_pre, up_pre = acc[0], acc[1]
    sigma = 1.0 / (1.0 + jnp.exp(-gate_pre))
    acc[0] = up_pre * sigma * (1.0 + gate_pre * (1.0 - sigma))
    acc[1] = gate_pre * sigma
    forward_last(2)
    hidden = acc[2]
    hid[0] = (hidden * acc[0]).astype(BF16)
    hid[1] = (hidden * acc[1]).astype(BF16)

    over = (((1,), (1,)), ((), ()))

    def held(block):
        away = lax.rem(z + nz - block, nz)
        low = jnp.where(away == 0, 0, 2 * away)
        return jnp.where(away < half, low, jnp.where(away == half, 1, 2 * (nz - away) + 1))

    def backward(p):
        term = None
        first, second = held(2 * p), held(2 * p + 1)
        for m in range(2):
            rhs = jnp.concatenate([wbuf[m, first], wbuf[m, second]], axis=0)
            part_sum = lax.dot_general(hid[m], rhs, over, preferred_element_type=F32)
            term = part_sum if term is None else term + part_sum
        return term

    def fold(dest, a, b):
        def put(r):
            o, q = r * 16, nx * 16 + r * 8
            dest(r)[0:16, :] = a[o : o + 16].astype(BF16)
            dest(r)[16:32, :] = b[o : o + 16].astype(BF16)
            dest(r)[32:48, :] = jnp.concatenate([a[q : q + 8], b[q : q + 8]], axis=0).astype(BF16)

        return put

    def near_copy(i, r):
        return pltpu.make_async_remote_copy(
            src_ref=near_out.at[i, r],
            dst_ref=near_in.at[i, r],
            send_sem=n_send.at[i, r],
            recv_sem=n_recv.at[i, r],
            device_id=back_to(r, -NEAR[i]),
            device_id_type=MESH,
        )

    def far_copy(h, r):
        return pltpu.make_async_remote_copy(
            src_ref=far_out.at[h, r],
            dst_ref=far_in.at[h, r],
            send_sem=f_send.at[h, r],
            recv_sem=f_recv.at[h, r],
            device_id=back_to(r, -NEAR[3 + h]),
            device_id_type=MESH,
        )

    across = (2, 1, 3, 0)
    quad = [lax.rem(y + k, QUADS) for k in range(QUADS)]
    for h in range(2):
        a = backward(2 * quad[2] + h)
        put = fold(lambda r: far_out.at[h, r], a[:, :128], a[:, 128:])
        for r in across:
            put(r)
            start(far_copy(h, r))
    for i, k in ((0, 0), (1, 1), (2, 3)):
        a, b = backward(2 * quad[k]), backward(2 * quad[k] + 1)
        put = fold(lambda r: near_out.at[i, r] if r or i else near_in.at[0, 0], a, b)
        for r in across:
            put(r)
            if r or i:
                start(near_copy(i, r))

    sums = []
    for h in range(2):
        rows = []
        for r in range(nx):
            far_copy(h, r).wait_recv()
            rest = far_in[h, r, 32:48, :].astype(F32)
            rest = jnp.concatenate([rest[0:8], rest[8:16]], axis=1)
            rows += [
                jnp.concatenate([far_in[h, r, 0:16, :], far_in[h, r, 16:32, :]], axis=1),
                jnp.concatenate([rest, jnp.zeros_like(rest)], axis=0).astype(BF16),
            ]
        sums.append(
            jnp.dot(
                spread[3 + h, 0], jnp.concatenate(rows, axis=0), preferred_element_type=F32
            )
        )
    for i in (0, 1, 2):
        for r in range(nx):
            if r or i:
                near_copy(i, r).wait_recv()
        for h in range(2):
            rows = []
            for r in range(nx):
                rows += [near_in[i, r, h * 16 : h * 16 + 16, :], near_in[i, r, 32:48, :]]
            sums[h] += jnp.dot(
                spread[i, h], jnp.concatenate(rows, axis=0), preferred_element_type=F32
            )
    for h in range(2):
        part[:, h * 256 : h * 256 + 256] = sums[h].astype(BF16)

    def rows_of(i):
        return pl.ds(pl.multiple_of(y_at[i] * 16, 16), 16)

    place_out = out_ref.at[
        lax.div(y, QUADS), :, pl.ds(pl.multiple_of(quad[0] * 512, 512), 512)
    ]

    def y_copy(i):
        return pltpu.make_async_remote_copy(
            src_ref=part.at[rows_of(i), :],
            dst_ref=place_out,
            send_sem=y_send.at[i],
            recv_sem=y_recv.at[i],
            device_id=back_to(0, i),
            device_id_type=MESH,
        )

    for i in (4, 3, 5, 2, 6, 1, 7):
        start(y_copy(i))
    kept = pltpu.make_async_copy(part.at[rows_of(0), :], place_out, y_send.at[0])
    kept.start()
    for i in range(1, ny):
        y_copy(i).wait_recv()
    kept.wait()
    for copy in sent:
        copy.wait_send()


def solution(mesh):
    nz, nx, ny = mesh.shape["dp"] // 2, mesh.shape["node"], mesh.shape["innode"]

    def local(tokens, routes, route_gates, out_grad, gate_weight, up_weight, down_weight):
        n_tok, width = tokens.shape
        units = gate_weight.shape[2]
        rows = nx * ROWS
        assert (nx, ny, nz, width, n_tok) == (4, 8, 16, 2048, 128)
        half = nz // 2
        any_space = pl.BlockSpec(memory_space=pl.ANY)
        dma = pltpu.SemaphoreType.DMA
        halves = pl.pallas_call(
            functools.partial(body, nz, nx, ny),
            out_shape=jax.ShapeDtypeStruct((2, n_tok // ny, width), BF16),
            in_specs=[any_space] * 7,
            out_specs=any_space,
            scratch_shapes=[
                pltpu.VMEM((3, nz, 128, units), BF16),
                pltpu.VMEM((n_tok, width), BF16),
                pltpu.VMEM((n_tok, width), BF16),
                pltpu.VMEM(routes.shape[::-1], jnp.int32),
                pltpu.VMEM(route_gates.shape[::-1], F32),
                pltpu.VMEM((nx, 48, width), BF16),
                pltpu.VMEM((nx - 1, 48, width), BF16),
                pltpu.VMEM((2, rows, width), BF16),
                pltpu.VMEM((3, rows, units), F32),
                pltpu.VMEM((2, rows, units), BF16),
                pltpu.VMEM((5, 2, n_tok, nx * SLOT), BF16),
                pltpu.VMEM((3, nx, 48, 256), BF16),
                pltpu.VMEM((3, nx, 48, 256), BF16),
                pltpu.VMEM((2, nx, 48, 128), BF16),
                pltpu.VMEM((2, nx, 48, 128), BF16),
                pltpu.VMEM((n_tok, 512), BF16),
                dma((4,)),
                dma((3,)),
                dma((half + 1, 3, 2)),
                dma((half + 1, 3, 2)),
                dma((2,)),
                dma((2,)),
                dma((half + 1, 3)),
                dma((half + 1, 3)),
                dma((2, nx)),
                dma((3, nx)),
                dma((3, nx)),
                dma((2, nx)),
                dma((2, nx)),
                dma((ny,)),
                dma((ny,)),
            ],
            compiler_params=pltpu.CompilerParams(
                collective_id=0, has_side_effects=True, vmem_limit_bytes=60 * 1024 * 1024
            ),
            cost_estimate=pl.CostEstimate(
                flops=10 * rows * width * units,
                bytes_accessed=16 * 1024 * 1024,
                transcendentals=rows * units,
            ),
            name="moe_input_grad",
        )(tokens, routes.T, route_gates.T, out_grad, gate_weight, up_weight, down_weight)
        return (halves[0].astype(F32) + halves[1].astype(F32)).astype(BF16)

    return jax.shard_map(
        local,
        mesh=mesh,
        in_specs=(
            P(("dp", "node"), None),
            P(("dp", "node"), None),
            P(("dp", "node"), None),
            P(("dp", "node"), None),
            P(("node", "innode"), "dp", None),
            P(("node", "innode"), "dp", None),
            P(("node", "innode"), "dp", None),
        ),
        out_specs=P(("dp", "node", "innode"), None),
        check_vma=False,
    )
```

```python
import functools

import jax
import jax.numpy as jnp
from jax import lax
from jax.experimental import pallas as pl
from jax.experimental.pallas import tpu as pltpu
from jax.sharding import PartitionSpec as P

MESH = pl.DeviceIdType.MESH
F32 = jnp.float32
BF16 = jnp.bfloat16

ROWS = 24
SLOT = 32
NEAR = (0, -1, 1, 2, -2)
QUADS = 4


def body(
    nz, nx, ny,
    tok_hbm, routes_hbm, gates_hbm, grad_hbm, gate_hbm, up_hbm, down_hbm,
    out_ref,
    wbuf, tok, grd, rts, gts, xs, xr, lhs, acc, hid, spread, near_out, near_in, far_out, far_in, part,
    in_sem, own_sem, z_send, z_recv, e_send, e_recv, p_send, p_recv, x_sem, n_send, n_recv, f_send, f_recv, y_send, y_recv,
):
    half = nz // 2
    pairs = nz // 2
    dp = lax.axis_index("dp")
    x = lax.axis_index("node")
    y = lax.axis_index("innode")
    z, c = lax.div(dp, 2), lax.rem(dp, 2)
    nxt = lax.rem(z + 1, nz) * 2 + c
    prv = lax.rem(z + nz - 1, nz) * 2 + c
    ring = ({"dp": nxt}, {"dp": prv})
    partner = {"dp": z * 2 + 1 - c}
    cross = ({"dp": nxt + 1 - 2 * c}, {"dp": prv + 1 - 2 * c})
    x_to = [{"node": lax.rem(x + r, nx)} for r in range(nx)]
    y_at = [lax.rem(y + i, ny) for i in range(ny)]

    def back_to(r, step):
        return {"node": lax.rem(x + nx - r, nx), "innode": y_at[step % ny]}


    def mine(m, pos, count):
        return wbuf.at[m, pl.ds(pos, count), pl.ds(pl.multiple_of(c * 64, 64), 64), :]

    def piece(m, pos, s, d):
        if s == half:
            return wbuf.at[m, pos, pl.ds(pl.multiple_of(c * 64 + d * 32, 32), 32), :]
        return wbuf.at[m, pos, pl.ds(pl.multiple_of(c * 64, 64), 64), :]

    own = []
    for m, ref in enumerate((gate_hbm, up_hbm, down_hbm)):
        copy = pltpu.make_async_copy(ref, mine(m, 0, 1), own_sem.at[m])
        copy.start()
        own.append(copy)
    ins = []
    for i, (a, b) in enumerate(
        ((routes_hbm, rts), (gates_hbm, gts), (tok_hbm, tok), (grad_hbm, grd))
    ):
        copy = pltpu.make_async_copy(a, b, in_sem.at[i])
        copy.start()
        ins.append(copy)

    barrier = pltpu.get_barrier_semaphore()
    peers = [ring[0], ring[1], partner, cross[0], cross[1]]
    peers += [back_to(r, i) for r in range(nx) for i in (-2, -1, 0, 1, 2) if r or i]
    peers += [back_to(0, i) for i in range(3, ny - 2)]
    for peer in peers:
        pl.semaphore_signal(barrier, inc=1, device_id=peer, device_id_type=MESH)
    pl.semaphore_wait(barrier, len(peers))

    def z_copy(s, m, d):
        return pltpu.make_async_remote_copy(
            src_ref=piece(m, place(s - 1, d), s, d),
            dst_ref=piece(m, place(s, d), s, d),
            send_sem=z_send.at[s, m, d],
            recv_sem=z_recv.at[s, m, d],
            device_id=ring[d],
            device_id_type=MESH,
        )

    def e_copy(d):
        return pltpu.make_async_remote_copy(
            src_ref=piece(2, place(half - 1, d), half, d),
            dst_ref=piece(2, place(half, d), half, d),
            send_sem=e_send.at[d],
            recv_sem=e_recv.at[d],
            device_id=cross[d],
            device_id_type=MESH,
        )

    def p_copy(s, m):
        ref = mine(m, 2 * s, 2) if 0 < s < half else mine(m, 0 if s == 0 else 1, 1)
        return pltpu.make_async_remote_copy(
            src_ref=ref,
            dst_ref=ref,
            send_sem=p_send.at[s, m],
            recv_sem=p_recv.at[s, m],
            device_id=partner,
            device_id_type=MESH,
        )

    sent = []

    def start(copy):
        copy.start()
        sent.append(copy)

    def place(s, d):
        return 0 if s == 0 else (1 if s == half else 2 * s + d)

    def service(s):
        for m in range(3):
            for d in range(2):
                z_copy(s, m, d).wait_recv()
                if s < half:
                    start(z_copy(s + 1, m, d))
                if s + 1 == half and m == 2:
                    start(e_copy(d))
            if s < half or m < 2:
                start(p_copy(s, m))

    for m in range(3):
        own[m].wait()
        for d in range(2):
            start(z_copy(1, m, d))
    for m in range(3):
        start(p_copy(0, m))

    ins[0].wait()
    ins[1].wait()
    n_tok = rts.shape[1]
    lanes = nx * SLOT
    line = lax.broadcasted_iota(jnp.int32, (lanes, n_tok), 0)
    slot = line & (SLOT - 1)
    slot1 = jnp.where(slot < 16, slot, jnp.where(slot >= 24, slot - 8, -1))
    group = x + (line >> 5)
    group = jnp.where(group >= nx, group - nx, group)
    earlier = (
        lax.broadcasted_iota(jnp.int32, (n_tok, n_tok), 0)
        < lax.broadcasted_iota(jnp.int32, (n_tok, n_tok), 1)
    ).astype(F32).astype(BF16)

    def find(step):
        expert = group * ny + y_at[step % ny]
        hit = jnp.zeros((lanes, n_tok), F32)
        weight = jnp.zeros((lanes, n_tok), F32)
        for k in range(rts.shape[0]):
            same = rts[k : k + 1, :] == expert
            hit = jnp.where(same, 1.0, hit)
            weight = jnp.where(same, gts[k : k + 1, :], weight)
        rank = jnp.dot(hit.astype(BF16), earlier, preferred_element_type=F32)
        own0 = jnp.where(rank == slot.astype(F32), hit, 0.0)
        own1 = jnp.where(rank == slot1.astype(F32), hit, 0.0)
        return own0, own1, weight

    def keep(i, rows):
        for h in range(2):
            spread[i, h] = jnp.transpose(rows[h]).astype(BF16)

    own_rows = find(0)
    pick = own_rows[0].astype(BF16)
    scale = jnp.sum(own_rows[0] * own_rows[2], axis=1, keepdims=True)

    ins[2].wait()
    ins[3].wait()
    for p in range(pairs):
        first = pl.multiple_of(lax.rem(z + nz - p, nz) * 128, 128)
        second = pl.multiple_of(lax.rem(z + (half if p == 0 else p), nz) * 128, 128)
        cols = pl.ds(p * 256, 256)
        a = jnp.concatenate([tok[:, pl.ds(first, 128)], tok[:, pl.ds(second, 128)]], axis=1)
        b = jnp.concatenate([grd[:, pl.ds(first, 128)], grd[:, pl.ds(second, 128)]], axis=1)
        a = jnp.dot(pick, a, preferred_element_type=F32)
        b = jnp.dot(pick, b, preferred_element_type=F32) * scale
        for r in range(nx):
            o = r * SLOT
            xs[r, 0:16, cols] = a[o : o + 16].astype(BF16)
            xs[r, 16:32, cols] = b[o : o + 16].astype(BF16)
            xs[r, 32:48, cols] = jnp.concatenate(
                [a[o + 16 : o + 24], b[o + 16 : o + 24]], axis=0
            ).astype(BF16)
    x_copies = []
    for r in range(1, nx):
        copy = pltpu.make_async_remote_copy(
            src_ref=xs.at[r],
            dst_ref=xr.at[r - 1],
            send_sem=x_sem.at[0, r],
            recv_sem=x_sem.at[1, r],
            device_id=x_to[r],
            device_id_type=MESH,
        )
        start(copy)
        x_copies.append(copy)

    keep(0, own_rows)

    def assemble():
        for copy in x_copies:
            copy.wait_recv()
        got = [xs.at[0]] + [xr.at[r - 1] for r in range(1, nx)]
        for r in range(nx):
            lhs[0, r * 16 : r * 16 + 16, :] = got[r][0:16, :]
            lhs[1, r * 16 : r * 16 + 16, :] = got[r][16:32, :]
        for r in range(0, nx, 2):
            a = got[r][32:48, :].astype(F32)
            b = got[r + 1][32:48, :].astype(F32)
            o = nx * 16 + r * 8
            lhs[0, o : o + 16, :] = jnp.concatenate([a[0:8], b[0:8]], axis=0).astype(BF16)
            lhs[1, o : o + 16, :] = jnp.concatenate([a[8:16], b[8:16]], axis=0).astype(BF16)

    def add(m, pos, count, fresh=False):
        term = jnp.dot(
            lhs[m // 2, :, pos * 128 : (pos + count) * 128],
            wbuf[m, pos : pos + count].reshape(count * 128, wbuf.shape[3]),
            preferred_element_type=F32,
        )
        if fresh:
            acc[m] = term
        else:
            acc[m] += term

    def forward(p, m):
        p_copy(p, m).wait_recv()
        add(m, 2 * p, 2, p == 1)

    def forward_last(m):
        if m < 2:
            p_copy(half, m).wait_recv()
            p_copy(0, m).wait_recv()
            add(m, 0, 2)
        else:
            e_copy(0).wait_recv()
            e_copy(1).wait_recv()
            add(m, 1, 1)

    wait_steps = min(3, half - 1)
    ready = []
    for s in range(1, half):
        service(s)
        if s == wait_steps:
            assemble()
        if s >= wait_steps:
            while ready:
                p = ready.pop(0)
                for m in range(3):
                    forward(p, m)
            if s > wait_steps:
                i = s - wait_steps
                keep(i, find(NEAR[i]))
        ready.append(s)
    for p in ready:
        for m in range(3):
            forward(p, m)
    p_copy(0, 2).wait_recv()
    add(2, 0, 1)
    service(half)
    forward_last(0)
    forward_last(1)
    gate_pre, up_pre = acc[0], acc[1]
    sigma = 1.0 / (1.0 + jnp.exp(-gate_pre))
    acc[0] = up_pre * sigma * (1.0 + gate_pre * (1.0 - sigma))
    acc[1] = gate_pre * sigma
    forward_last(2)
    hidden = acc[2]
    hid[0] = (hidden * acc[0]).astype(BF16)
    hid[1] = (hidden * acc[1]).astype(BF16)

    over = (((1,), (1,)), ((), ()))

    def held(block):
        away = lax.rem(z + nz - block, nz)
        low = jnp.where(away == 0, 0, 2 * away)
        return jnp.where(away < half, low, jnp.where(away == half, 1, 2 * (nz - away) + 1))

    def backward(p):
        term = None
        first, second = held(2 * p), held(2 * p + 1)
        for m in range(2):
            rhs = jnp.concatenate([wbuf[m, first], wbuf[m, second]], axis=0)
            part_sum = lax.dot_general(hid[m], rhs, over, preferred_element_type=F32)
            term = part_sum if term is None else term + part_sum
        return term

    def fold(dest, a, b):
        def put(r):
            o, q = r * 16, nx * 16 + r * 8
            dest(r)[0:16, :] = a[o : o + 16].astype(BF16)
            dest(r)[16:32, :] = b[o : o + 16].astype(BF16)
            dest(r)[32:48, :] = jnp.concatenate([a[q : q + 8], b[q : q + 8]], axis=0).astype(BF16)

        return put

    def near_copy(i, r):
        return pltpu.make_async_remote_copy(
            src_ref=near_out.at[i, r],
            dst_ref=near_in.at[i, r],
            send_sem=n_send.at[i, r],
            recv_sem=n_recv.at[i, r],
            device_id=back_to(r, -NEAR[i]),
            device_id_type=MESH,
        )

    def far_copy(h, r):
        return pltpu.make_async_remote_copy(
            src_ref=far_out.at[h, r],
            dst_ref=far_in.at[h, r],
            send_sem=f_send.at[h, r],
            recv_sem=f_recv.at[h, r],
            device_id=back_to(r, -NEAR[3 + h]),
            device_id_type=MESH,
        )

    across = (2, 1, 3, 0)
    quad = [lax.rem(y + k, QUADS) for k in range(QUADS)]
    def send_near(i, k):
        a, b = backward(2 * quad[k]), backward(2 * quad[k] + 1)
        put = fold(lambda r: near_out.at[i, r] if r or i else near_in.at[0, 0], a, b)
        for r in across:
            put(r)
            if r or i:
                start(near_copy(i, r))

    send_near(0, 0)
    for h in range(2):
        a = backward(2 * quad[2] + h)
        put = fold(lambda r: far_out.at[h, r], a[:, :128], a[:, 128:])
        for r in across:
            put(r)
            start(far_copy(h, r))
    send_near(1, 1)
    send_near(2, 3)

    sums = []
    for h in range(2):
        rows = []
        for r in range(nx):
            far_copy(h, r).wait_recv()
            rest = far_in[h, r, 32:48, :].astype(F32)
            rest = jnp.concatenate([rest[0:8], rest[8:16]], axis=1)
            rows += [
                jnp.concatenate([far_in[h, r, 0:16, :], far_in[h, r, 16:32, :]], axis=1),
                jnp.concatenate([rest, jnp.zeros_like(rest)], axis=0).astype(BF16),
            ]
        sums.append(
            jnp.dot(
                spread[3 + h, 0], jnp.concatenate(rows, axis=0), preferred_element_type=F32
            )
        )
    for i in (0, 1, 2):
        for r in range(nx):
            if r or i:
                near_copy(i, r).wait_recv()
        for h in range(2):
            rows = []
            for r in range(nx):
                rows += [near_in[i, r, h * 16 : h * 16 + 16, :], near_in[i, r, 32:48, :]]
            sums[h] += jnp.dot(
                spread[i, h], jnp.concatenate(rows, axis=0), preferred_element_type=F32
            )
    for h in range(2):
        part[:, h * 256 : h * 256 + 256] = sums[h].astype(BF16)

    def rows_of(i):
        return pl.ds(pl.multiple_of(y_at[i] * 16, 16), 16)

    place_out = out_ref.at[
        lax.div(y, QUADS), :, pl.ds(pl.multiple_of(quad[0] * 512, 512), 512)
    ]

    def y_copy(i):
        return pltpu.make_async_remote_copy(
            src_ref=part.at[rows_of(i), :],
            dst_ref=place_out,
            send_sem=y_send.at[i],
            recv_sem=y_recv.at[i],
            device_id=back_to(0, i),
            device_id_type=MESH,
        )

    for i in (4, 3, 5, 2, 6, 1, 7):
        start(y_copy(i))
    kept = pltpu.make_async_copy(part.at[rows_of(0), :], place_out, y_send.at[0])
    kept.start()
    for i in range(1, ny):
        y_copy(i).wait_recv()
    kept.wait()
    for copy in sent:
        copy.wait_send()


def solution(mesh):
    nz, nx, ny = mesh.shape["dp"] // 2, mesh.shape["node"], mesh.shape["innode"]

    def local(tokens, routes, route_gates, out_grad, gate_weight, up_weight, down_weight):
        n_tok, width = tokens.shape
        units = gate_weight.shape[2]
        rows = nx * ROWS
        assert (nx, ny, nz, width, n_tok) == (4, 8, 16, 2048, 128)
        half = nz // 2
        any_space = pl.BlockSpec(memory_space=pl.ANY)
        dma = pltpu.SemaphoreType.DMA
        halves = pl.pallas_call(
            functools.partial(body, nz, nx, ny),
            out_shape=jax.ShapeDtypeStruct((2, n_tok // ny, width), BF16),
            in_specs=[any_space] * 7,
            out_specs=any_space,
            scratch_shapes=[
                pltpu.VMEM((3, nz, 128, units), BF16),
                pltpu.VMEM((n_tok, width), BF16),
                pltpu.VMEM((n_tok, width), BF16),
                pltpu.VMEM(routes.shape[::-1], jnp.int32),
                pltpu.VMEM(route_gates.shape[::-1], F32),
                pltpu.VMEM((nx, 48, width), BF16),
                pltpu.VMEM((nx - 1, 48, width), BF16),
                pltpu.VMEM((2, rows, width), BF16),
                pltpu.VMEM((3, rows, units), F32),
                pltpu.VMEM((2, rows, units), BF16),
                pltpu.VMEM((5, 2, n_tok, nx * SLOT), BF16),
                pltpu.VMEM((3, nx, 48, 256), BF16),
                pltpu.VMEM((3, nx, 48, 256), BF16),
                pltpu.VMEM((2, nx, 48, 128), BF16),
                pltpu.VMEM((2, nx, 48, 128), BF16),
                pltpu.VMEM((n_tok, 512), BF16),
                dma((4,)),
                dma((3,)),
                dma((half + 1, 3, 2)),
                dma((half + 1, 3, 2)),
                dma((2,)),
                dma((2,)),
                dma((half + 1, 3)),
                dma((half + 1, 3)),
                dma((2, nx)),
                dma((3, nx)),
                dma((3, nx)),
                dma((2, nx)),
                dma((2, nx)),
                dma((ny,)),
                dma((ny,)),
            ],
            compiler_params=pltpu.CompilerParams(
                collective_id=0, has_side_effects=True, vmem_limit_bytes=60 * 1024 * 1024
            ),
            cost_estimate=pl.CostEstimate(
                flops=10 * rows * width * units,
                bytes_accessed=16 * 1024 * 1024,
                transcendentals=rows * units,
            ),
            name="moe_input_grad",
        )(tokens, routes.T, route_gates.T, out_grad, gate_weight, up_weight, down_weight)
        return (halves[0].astype(F32) + halves[1].astype(F32)).astype(BF16)

    return jax.shard_map(
        local,
        mesh=mesh,
        in_specs=(
            P(("dp", "node"), None),
            P(("dp", "node"), None),
            P(("dp", "node"), None),
            P(("dp", "node"), None),
            P(("node", "innode"), "dp", None),
            P(("node", "innode"), "dp", None),
            P(("node", "innode"), "dp", None),
        ),
        out_specs=P(("dp", "node", "innode"), None),
        check_vma=False,
    )
```
